32 devices in a mesh: mesh: 8 (over z, x), vec: 4 (over y, core).
Axes of the slice: x: 2, y: 2, z: 4, core: 2. Of those that a mesh axis runs over, the one named last changes fastest.
Arguments:
- panel: float32 [65536, 128], P('mesh', 'vec'), may hold values from -6 to 6
- orient: int32 [65536], P('mesh'), may hold values from -1 to 1, as said below
- mass: float32 [65536], P('mesh'), may hold values from 0.5 to 2
- stiff_diag: bfloat16 [512, 128, 128], P('mesh'), may hold values from -0.05 to 4, as said below
- near_coupling: bfloat16 [512, 128, 128], P('mesh'), may hold values from -0.1796875 to 0.1796875
- far_coupling: bfloat16 [512, 128, 128], P('mesh'), may hold values from -0.1796875 to 0.1796875
Outputs:
- filtered: float32 [65536, 128], P('mesh', 'vec')
- ritz_stiff: float32 [128, 128], P('vec', 'mesh')
- ritz_mass: float32 [128, 128], P('vec', 'mesh')
The draws below stay inside these ranges and needn't reach their ends.
Inputs may be any that keep to these rules, and one draw needn't show every extreme that they name: `orient`: every entry is +1 or -1. `stiff_diag`: each block is symmetric; its diagonal entries lie from 2 to 4 and its off-diagonal entries have magnitude at most 0.05.
All inputs are finite; a program needn't handle non-finite values.
Results may differ from the reference program's by a relative error of at most 0.0035.
Values may be sent and summed in bfloat16 or wider, within the bound.
No kernel may reach another device: no remote copies, remote signals or barrier semaphores. Data moves between devices by JAX's collectives and lax.ppermute only.
A program may use at most 64 MiB of HBM per device.

```python
import math
import jax
import jax.numpy as jnp
from jax import lax

BS = 128
VECS = 128
SPAN = 32
DEGREE = 4
APPS = 2
NBLK = 512
EDGES = 65536


def draw_orient(key, part):
    return (2 * jax.random.randint(key, (NBLK * BS,), 0, 2) - 1).astype(jnp.int32)


def draw_stiff_diag(key, part):
    first, second = jax.random.split(key)
    noise = jnp.clip(0.03 * jax.random.normal(first, (NBLK, BS, BS), jnp.float32), -0.049, 0.049)
    symmetric = 0.5 * (noise + jnp.swapaxes(noise, 1, 2))
    diagonal = jax.random.uniform(second, (NBLK, BS, 1), jnp.float32, 2.0, 4.0)
    identity = jnp.eye(BS, dtype=jnp.float32)
    return (symmetric * (1.0 - identity) + identity * diagonal).astype(jnp.bfloat16)


def spiked(result, key, source, target, blocks, factor):
    owner, partner = [(jnp.arange(result.shape[axis_at]) // (result.shape[axis_at] // blocks)).reshape([-1 if axis == axis_at else 1 for axis in range(result.ndim)]) for axis_at in (source, target)]
    chosen = jax.random.permutation(key, blocks)[partner]
    strong = (owner == chosen) | (owner == (partner + blocks // 2) % blocks)
    return jnp.where(strong, factor * result, result)


def shard_levels(key, extent, shards, low, largest):
    level, own = 1.0, jax.random.fold_in(key, 6)
    for position, parts in shards:
        heights = jnp.exp(jax.random.uniform(jax.random.fold_in(own, position), (parts,), jnp.float32, low / len(shards), largest / len(shards)))
        level = level * jnp.repeat(heights, extent[position] // parts).reshape([-1 if axis == position else 1 for axis in range(len(extent))])
    return level


def gaussian(stream_key, dims, width, reach, shards=(), kind=jnp.bfloat16):
    entries = jax.random.normal(stream_key, dims, jnp.float32) * width
    if len(shards) > 0:
        entries = shard_levels(stream_key, dims, shards, -0.22, 0.18) * entries
    return jnp.clip(entries, min=-reach, max=reach).astype(kind)


def noise_with(own_key, extent, scale, reach, pieces, heavy, kind=jnp.bfloat16):
    entries = scale * jax.random.normal(own_key, extent, jnp.float32)
    if pieces:
        entries = entries * shard_levels(own_key, extent, pieces, -0.22, 0.18)
    return jnp.clip(spiked(entries, jax.random.fold_in(own_key, 3), *heavy), -reach, reach).astype(kind)


def setup_inputs(seed: int = 0) -> dict:
    seeds = jax.random.split(jax.random.key(seed), 7)
    panel = noise_with(seeds[0], (EDGES, VECS), 1.0, 6.0, ((0, 8), (1, 4)), (0, 1, 8, 2.0), jnp.float32)
    orient = draw_orient(jax.random.fold_in(seeds[6], 71), 0)
    mass = jnp.clip(jnp.exp(math.log(2.0) - 1.3862944 * jax.random.uniform(seeds[2], (EDGES,), jnp.float32) ** shard_levels(seeds[2], (EDGES,), ((0, 8),), -0.2, 0.2)), 0.5, 2.0)
    stiff_diag = draw_stiff_diag(jax.random.fold_in(seeds[6], 71), 0)
    near_coupling = gaussian(seeds[4], (NBLK, BS, BS), 0.03, 0.1796875, ((0, 8),))
    far_coupling = gaussian(seeds[5], (NBLK, BS, BS), 0.03, 0.1796875, ((0, 8),))
    return dict(panel=panel, orient=orient, mass=mass, stiff_diag=stiff_diag, near_coupling=near_coupling, far_coupling=far_coupling)


filter_center = 6.0
filter_radius = 8.0

def shift_down(values, amount):
    pad = jnp.zeros((amount,) + values.shape[1:], values.dtype)
    return jnp.concatenate([pad, values[:-amount]], axis=0)

def shift_up(values, amount):
    pad = jnp.zeros((amount,) + values.shape[1:], values.dtype)
    return jnp.concatenate([values[amount:], pad], axis=0)

def reference(panel, orient, mass, stiff_diag, near_coupling, far_coupling):
    highest = lax.Precision.HIGHEST
    scale = orient.astype(jnp.float32) / jnp.sqrt(mass)
    diag_full = stiff_diag.astype(jnp.float32)
    near_full = near_coupling.astype(jnp.float32)
    far_full = far_coupling.astype(jnp.float32)

    def operate(field):
        scaled = (scale[:, None] * field).astype(jnp.bfloat16).astype(jnp.float32)
        blocks = scaled.reshape(NBLK, BS, VECS)
        total = jnp.einsum('bij,bjc->bic', diag_full, blocks, precision=highest)
        total = total + jnp.einsum('bij,bjc->bic', near_full, shift_down(blocks, 1), precision=highest)
        total = total + shift_up(jnp.einsum('bji,bjc->bic', near_full, blocks, precision=highest), 1)
        total = total + jnp.einsum('bij,bjc->bic', far_full, shift_down(blocks, SPAN), precision=highest)
        total = total + shift_up(jnp.einsum('bji,bjc->bic', far_full, blocks, precision=highest), SPAN)
        return scale[:, None] * total.reshape(EDGES, VECS)

    def chebyshev(start):
        before = start
        current = (operate(start) - filter_center * start) / filter_radius
        for step in range(DEGREE - 1):
            following = 2.0 * (operate(current) - filter_center * current) / filter_radius - before
            before, current = (current, following)
        return current
    filtered = panel
    for application in range(APPS):
        filtered = chebyshev(filtered)
    image = operate(filtered)
    filtered_b = filtered.astype(jnp.bfloat16)
    image_b = image.astype(jnp.bfloat16)
    ritz_stiff = jnp.dot(filtered_b.T, image_b, preferred_element_type=jnp.float32)
    ritz_mass = jnp.dot(filtered_b.T, filtered_b, preferred_element_type=jnp.float32)
    return (filtered, ritz_stiff, ritz_mass)
```

```python
import functools

import jax
import jax.numpy as jnp
from jax import lax
from jax.experimental import pallas as pl
from jax.experimental.pallas import tpu as pltpu
from jax.sharding import PartitionSpec as P

SPAN = 32
DEGREE = 4
APPS = 2
CENTER = 6.0
RADIUS = 8.0

BOTH = ("mesh", "vec")
F32 = jnp.float32
BF16 = jnp.bfloat16
VMEM_LIMIT = 24 * 1024 * 1024


def gray(t):
    return t ^ (t >> 1)


class Plan:
    def __init__(self, meshes, vecs, blocks, width, columns):
        self.meshes, self.vecs, self.blocks, self.width, self.columns = meshes, vecs, blocks, width, columns
        self.ring = [(0, gray(t)) for t in range(vecs)] + [(1, gray(t)) for t in reversed(range(vecs))]
        self.segments = 2 * vecs
        self.seg = {place: s for s, place in enumerate(self.ring)}
        self.layers = meshes // 2
        self.own = blocks // SPAN
        self.rows = 2 * self.own
        self.run = SPAN // self.segments
        self.half = self.run // 2
        self.lanes = self.run * width
        self.vectors = vecs * columns
        self.inner, self.outer = {}, {}
        for i in range(self.rows):
            for p in range(self.run):
                self.inner["D", i, p] = len(self.inner)
        for i in range(self.rows):
            for p in range(1, self.run):
                self.inner["N", i, p] = len(self.inner)
        for i in range(1, self.rows):
            for p in range(self.run):
                self.inner["F", i, p] = len(self.inner)
        for p in range(self.run):
            self.outer["F", 0, p] = len(self.outer)
        for p in range(self.run):
            self.outer["F", self.rows, p] = len(self.outer)
        for i in range(self.rows):
            self.outer["N", i, 0] = len(self.outer)
            self.outer["N", i, self.run] = len(self.outer)
        for i in (0, self.rows - 1, self.rows):
            self.outer["N", i, self.half] = len(self.outer)
        self.n_first = self.run + 2
        self.n_rest = self.own * self.run + self.own * (self.run + 1) + (self.own - 1) * self.run

    def received(self, kind, r, p):
        if kind == "D":
            return 1, r * self.run + p
        if kind == "N":
            return 1, self.own * self.run + r * (self.run + 1) + p
        if r == 0:
            return 0, p
        return 1, self.own * self.run + self.own * (self.run + 1) + (r - 1) * self.run + p

    def swap(self, x, partner):
        pairs = []
        for m in range(self.meshes):
            for v in range(self.vecs):
                to, at = partner(m, v)
                pairs.append((m * self.vecs + v, to * self.vecs + at))
        return lax.ppermute(x, BOTH, pairs)

    def layer_a(self, m, v):
        to = m ^ 2
        return (to, v) if to < self.meshes else (m, v ^ 1)

    def layer_b(self, m, v):
        z = m // 2
        to = m + 2 if z % 2 else m - 2
        return (to, v) if 0 <= to < self.meshes else (m, v ^ 1)

    def ring_swap(self, m, v):
        s = self.seg[m % 2, v]
        x, at = self.ring[(s + 1) % self.segments if s % 2 else (s - 1) % self.segments]
        return m - m % 2 + x, at

    def core_swap(self, m, v):
        return m, v ^ 1


def place(plan):
    m, v = lax.axis_index("mesh"), lax.axis_index("vec")
    x, z = lax.rem(m, 2), lax.div(m, 2)
    s = jnp.int32(0)
    for k, (a, b) in enumerate(plan.ring):
        s = s + jnp.where((x == a) & (v == b), k, 0)
    return x, z, v, s


def column(plan, s, p):
    return lax.rem(plan.run * s + (p - plan.half + SPAN), SPAN)


def pieces(plan, s):
    found = []
    for p in range(plan.run):
        j = (plan.run * s + p - plan.half) % SPAN
        if found and found[-1][1] + found[-1][2] == j:
            found[-1][2] += 1
        else:
            found.append([p, j, 1])
    return found


def dot(u, w):
    return lax.dot_general(u, w, (((1,), (0,)), ((), ())), preferred_element_type=F32)


def dot_turned(u, w):
    return lax.dot_general(u, w, (((1,), (1,)), ((), ())), preferred_element_type=F32)


def call(kernel, outs, ins, args, scratch=(), flops=0, moved=0, aliases=None):
    return pl.pallas_call(
        kernel,
        out_shape=outs,
        in_specs=ins,
        out_specs=jax.tree.map(lambda _: pl.BlockSpec(memory_space=pltpu.VMEM), outs),
        scratch_shapes=list(scratch),
        compiler_params=pltpu.CompilerParams(vmem_limit_bytes=VMEM_LIMIT),
        cost_estimate=pl.CostEstimate(flops=flops, bytes_accessed=moved, transcendentals=0),
    )(*args)


def vm(n):
    return [pl.BlockSpec(memory_space=pltpu.VMEM)] * n


def anywhere(n):
    return [pl.BlockSpec(memory_space=pl.ANY)] * n


def shape(*dims, dtype=F32):
    return jax.ShapeDtypeStruct(dims, dtype)


def prepare_kernel(plan, panel, orient, mass, diag, near, far, scale, chunks, own, first, rest, parts, sems):
    x, z, v, s = place(plan)
    other = plan.segments - 1 - s
    copies = []

    def fetch(src, r, seg, p, dst):
        at = r * SPAN + column(plan, seg, p)
        copy = pltpu.make_async_copy(src.at[at], dst, sems.at[len(copies)])
        copy.start()
        copies.append(copy)

    for p in range(plan.run):
        fetch(far, 0, other, p, first.at[p])
    fetch(near, 0, other, plan.half, first.at[plan.run])
    for r in range(plan.own):
        for p in range(plan.run):
            fetch(diag, r, other, p, rest.at[plan.received("D", r, p)[1]])
        for p in range(plan.run + 1):
            fetch(near, r, other, p, rest.at[plan.received("N", r, p)[1]])
        if r > 0:
            for p in range(plan.run):
                fetch(far, r, other, p, rest.at[plan.received("F", r, p)[1]])
    for p in range(plan.run):
        fetch(far, 0, s, p, own.at[p])
    fetch(near, 0, s, plan.half, own.at[plan.run])

    scale[...] = orient[...].astype(F32) * lax.rsqrt(mass[...])
    parts[...] = jnp.zeros_like(parts)
    count = plan.own * plan.run
    for r in range(plan.own):
        for p in range(plan.run):
            value = scale[pl.ds(r * SPAN + column(plan, other, p), 1), :]
            for part in range(3):
                rounded = value.astype(BF16).astype(F32)
                parts[pl.ds(part * count + r * plan.run + p, 1), :] = rounded
                value = value - rounded
    first[plan.run + 1] = parts[...].astype(BF16)

    for d in range(plan.segments):
        seg = plan.seg[d // plan.vecs, d % plan.vecs]
        for r in range(plan.own):
            for p, j, n in pieces(plan, seg):
                lo = (r * SPAN + j) * plan.width
                chunks[d, r, :, p * plan.width : (p + n) * plan.width] = panel[:, lo : lo + n * plan.width]
    for copy in copies:
        copy.wait()


def prepare(plan, panel, orient, mass, diag, near, far):
    w = plan.width
    n_copies = plan.n_first - 1 + plan.n_rest + plan.run + 1
    return call(
        functools.partial(prepare_kernel, plan),
        (
            shape(plan.blocks, w),
            shape(plan.segments, plan.own, plan.columns, plan.lanes),
            shape(plan.run + 1, w, w, dtype=BF16),
            shape(plan.n_first, w, w, dtype=BF16),
            shape(plan.n_rest, w, w, dtype=BF16),
        ),
        vm(3) + anywhere(3),
        (panel, orient, mass, diag, near, far),
        [pltpu.VMEM((w, w), F32), pltpu.SemaphoreType.DMA((n_copies,))],
        moved=4 << 20,
    )


def emit(plan, i, u, even_layer, even_seg, u_out, send_a, send_b, send_core, send_ring):
    u_out[i] = u
    if i in (0, plan.rows - 1):
        at_even, at_odd = (send_b, send_a) if i == 0 else (send_a, send_b)

        @pl.when(even_layer)
        def _():
            at_even[...] = u

        @pl.when(jnp.logical_not(even_layer))
        def _():
            at_odd[...] = u

    left, right = u[:, : plan.width], u[:, plan.lanes - plan.width :]

    @pl.when(even_seg)
    def _():
        send_core[i] = right
        send_ring[i] = left

    @pl.when(jnp.logical_not(even_seg))
    def _():
        send_core[i] = left
        send_ring[i] = right


def sends(plan):
    w = plan.width
    edge = shape(plan.vectors, plan.lanes, dtype=BF16)
    side = shape(plan.rows, plan.vectors, w, dtype=BF16)
    return (shape(plan.rows, plan.vectors, plan.lanes, dtype=BF16), edge, edge, side, side)


def begin_kernel(plan, got, scale_own, first, y_out, scale_out, u_out, send_a, send_b, send_core, send_ring):
    x, z, v, s = place(plan)
    even_layer, even_seg = lax.rem(z, 2) == 0, lax.rem(s, 2) == 0
    count = plan.own * plan.run
    parts = first[plan.run + 1].astype(F32)
    theirs = (parts[:count] + parts[count : 2 * count]) + parts[2 * count : 3 * count]
    for i in range(plan.rows):
        half, r = divmod(i, plan.own)
        for p in range(plan.run):
            mine = scale_own[pl.ds(r * SPAN + column(plan, s, p), 1), :]
            scale_out[pl.ds(i * plan.run + p, 1), :] = jnp.where(
                x == half, mine, theirs[r * plan.run + p : r * plan.run + p + 1]
            )
    for i in range(plan.rows):
        half, r = divmod(i, plan.own)
        for v in range(plan.vecs):
            y_out[i, v * plan.columns : (v + 1) * plan.columns, :] = got[half * plan.vecs + v, r]
        u = []
        for p in range(plan.run):
            row = scale_out[pl.ds(i * plan.run + p, 1), :]
            u.append((row * y_out[i, :, p * plan.width : (p + 1) * plan.width]).astype(BF16))
        emit(plan, i, jnp.concatenate(u, axis=1), even_layer, even_seg, u_out, send_a, send_b, send_core, send_ring)


def begin(plan, got, scale_own, first):
    return call(
        functools.partial(begin_kernel, plan),
        (shape(plan.rows, plan.vectors, plan.lanes), shape(plan.rows * plan.run, plan.width)) + sends(plan),
        vm(3),
        (got, scale_own, first),
        moved=4 << 20,
    )


def weights_kernel(plan, diag, near, far, first, rest, below, inner, outer, sems):
    x, z, v, s = place(plan)
    local = {"D": diag, "N": near, "F": far}
    waits = []
    for table, out in ((plan.inner, inner), (plan.outer, outer)):
        for (kind, i, p), k in table.items():
            dst, sem = out.at[k], sems.at[len(waits)]
            if i == plan.rows:
                pltpu.make_async_copy(below.at[p if kind == "F" else plan.run], dst, sem).start()
            else:
                half, r = divmod(i, plan.own)
                which, index = plan.received(kind, r, p)
                there = (first, rest)[which].at[index]
                here = local[kind].at[r * SPAN + column(plan, s, p)]

                @pl.when(x == half)
                def _():
                    pltpu.make_async_copy(here, dst, sem).start()

                @pl.when(x != half)
                def _():
                    pltpu.make_async_copy(there, dst, sem).start()

            waits.append(pltpu.make_async_copy(first.at[0], dst, sem))
    for copy in waits:
        copy.wait()


def weights(plan, diag, near, far, first, rest, below):
    w = plan.width
    return call(
        functools.partial(weights_kernel, plan),
        (shape(len(plan.inner), w, w, dtype=BF16), shape(len(plan.outer), w, w, dtype=BF16)),
        anywhere(6),
        (diag, near, far, first, rest, below),
        [pltpu.SemaphoreType.DMA((len(plan.inner) + len(plan.outer),))],
        moved=4 << 20,
    )


def inner_kernel(plan, factors, has_before, gram, *refs):
    a, b, c = factors
    refs = list(refs)
    u, y = refs[:2]
    before = refs[2] if has_before else None
    w_in, scale, part = refs[2 + has_before : 5 + has_before]
    x, z, v, s = place(plan)
    wrap = (s == 0).astype(jnp.int32)
    width, half, last = plan.width, plan.half, plan.rows - 1
    at = plan.inner
    for i in range(plan.rows):
        for p in range(plan.run):
            lanes = slice(p * width, (p + 1) * width)
            total = dot(u[i, :, lanes], w_in[at["D", i, p]])
            if p == half:
                if i > 0:
                    total += dot_turned(u[i - wrap, :, (p - 1) * width : p * width], w_in[at["N", i, p]])
            elif p > 0:
                total += dot_turned(u[i, :, (p - 1) * width : p * width], w_in[at["N", i, p]])
            if p + 1 == half:
                if i < last:
                    near = at["N", i, half] + wrap * (plan.run - 1)
                    total += dot(u[i + wrap, :, (p + 1) * width : (p + 2) * width], w_in[near])
            elif p + 1 < plan.run:
                total += dot(u[i, :, (p + 1) * width : (p + 2) * width], w_in[at["N", i, p + 1]])
            if i > 0:
                total += dot_turned(u[i - 1, :, lanes], w_in[at["F", i, p]])
            if i < last:
                total += dot(u[i + 1, :, lanes], w_in[at["F", i + 1, p]])
            result = (a * scale[pl.ds(i * plan.run + p, 1), :]) * total
            if b:
                result += b * y[i, :, lanes]
            if has_before:
                result += c * before[i, :, lanes]
            part[i, :, lanes] = result
    if gram:
        mass = refs[5 + has_before]
        total = jnp.zeros(mass.shape, F32)
        for i in range(plan.rows):
            rounded = y[i].astype(BF16)
            total += dot_turned(rounded, rounded)
        mass[...] = total


def inner(plan, factors, u, y, before, w_in, scale, gram=False):
    has_before = before is not None
    args = (u, y) + ((before,) if has_before else ()) + (w_in, scale)
    outs = (shape(plan.rows, plan.vectors, plan.lanes),)
    if gram:
        outs += (shape(plan.vectors, plan.vectors),)
    return call(
        functools.partial(inner_kernel, plan, factors, has_before, gram),
        outs,
        vm(len(args)),
        args,
        flops=130 << 20,
        moved=5 << 20,
    )


def halo_terms(plan, u, w_out, got_a, got_b, got_core, got_ring, top, bottom, left, right):
    x, z, v, s = place(plan)
    even_layer, even_seg, wrap = lax.rem(z, 2) == 0, lax.rem(s, 2) == 0, s == 0
    width, half, last, at = plan.width, plan.half, plan.rows - 1, plan.outer

    @pl.when(even_layer)
    def _():
        top[...] = got_b[...]
        bottom[...] = got_a[...]

    @pl.when(jnp.logical_not(even_layer))
    def _():
        top[...] = got_a[...]
        bottom[...] = got_b[...]

    @pl.when(z == 0)
    def _():
        top[...] = jnp.zeros_like(top)

    @pl.when(z == plan.layers - 1)
    def _():
        bottom[...] = jnp.zeros_like(bottom)

    @pl.when(even_seg)
    def _():
        left[...] = got_ring[...]
        right[...] = got_core[...]

    @pl.when(jnp.logical_not(even_seg))
    def _():
        left[...] = got_core[...]
        right[...] = got_ring[...]

    def row(i):
        found = {0: dot_turned(left[i], w_out[at["N", i, 0]])}
        found[plan.run - 1] = dot(right[i], w_out[at["N", i, plan.run]])

        def add(p, term):
            found[p] = found[p] + term if p in found else term

        if i == 0:
            for p in range(plan.run):
                add(p, dot_turned(top[:, p * width : (p + 1) * width], w_out[at["F", 0, p]]))
            lanes = slice((half - 1) * width, half * width)
            before = jnp.where(wrap, top[:, lanes].astype(F32), u[0, :, lanes].astype(F32)).astype(BF16)
            add(half, dot_turned(before, w_out[at["N", 0, half]]))
        if i == last:
            for p in range(plan.run):
                add(p, dot(bottom[:, p * width : (p + 1) * width], w_out[at["F", plan.rows, p]]))
            lanes = slice(half * width, (half + 1) * width)
            after = jnp.where(wrap, bottom[:, lanes].astype(F32), u[last, :, lanes].astype(F32)).astype(BF16)
            here, there = at["N", last, half], at["N", plan.rows, half]
            add(half - 1, dot(after, w_out[here + wrap.astype(jnp.int32) * (there - here)]))
        return found

    return row, even_layer, even_seg


def halo_scratch(plan):
    edge = pltpu.VMEM((plan.vectors, plan.lanes), BF16)
    side = pltpu.VMEM((plan.rows, plan.vectors, plan.width), BF16)
    return [edge, edge, side, side]


def finished_row(plan, i, part, scale, factor, terms):
    out = []
    for p in range(plan.run):
        value = part[i, :, p * plan.width : (p + 1) * plan.width]
        if p in terms:
            value += (factor * scale[pl.ds(i * plan.run + p, 1), :]) * terms[p]
        out.append(value)
    return out


def outer_kernel(plan, factor, leaving, part, u, w_out, scale, got_a, got_b, got_core, got_ring, *refs):
    refs = list(refs)
    y_out, u_out, send_a, send_b, send_core, send_ring = refs[:6]
    halos = refs[-4:]
    row, even_layer, even_seg = halo_terms(plan, u, w_out, got_a, got_b, got_core, got_ring, *halos)
    width = plan.width
    for i in range(plan.rows):
        values = finished_row(plan, i, part, scale, factor, row(i))
        rounded = []
        for p, value in enumerate(values):
            y_out[i, :, p * width : (p + 1) * width] = value
            rounded.append((scale[pl.ds(i * plan.run + p, 1), :] * value).astype(BF16))
        emit(plan, i, jnp.concatenate(rounded, axis=1), even_layer, even_seg, u_out, send_a, send_b, send_core, send_ring)
    if leaving:
        exit_core = refs[6]
        core = lax.rem(lax.axis_index("vec"), 2)
        for k in range(plan.segments // 2):
            half, chip = divmod(k, plan.vecs // 2)
            first = pl.multiple_of((2 * chip + 1 - core) * plan.columns, plan.columns)
            for r in range(plan.own):
                exit_core[k, r] = y_out[half * plan.own + r, pl.ds(first, plan.columns), :]


def exit_shape(plan, n):
    return shape(n, plan.own, plan.columns, plan.lanes)


def outer(plan, factor, part, u, w_out, scale, got, leaving=False):
    outs = (shape(plan.rows, plan.vectors, plan.lanes),) + sends(plan)
    if leaving:
        outs += (exit_shape(plan, plan.segments // 2),)
    args = (part, u, w_out, scale) + tuple(got)
    return call(
        functools.partial(outer_kernel, plan, factor, leaving),
        outs,
        vm(len(args)),
        args,
        halo_scratch(plan),
        flops=40 << 20,
        moved=5 << 20,
    )


def chip_order(plan):
    return [(dx, dy) for dx in range(2) for dy in range(plan.vecs // 2)]


def leave_kernel(plan, y, got_core, *outs):
    x, z, v, s = place(plan)
    core, chip = lax.rem(v, 2), lax.div(v, 2)
    for (dx, dy), out in zip(chip_order(plan), outs, strict=True):
        to_x = jnp.where(x == 1, 1 - dx, dx)
        to_chip = chip
        if dy:
            to_chip = jnp.int32(0)
            for k in range(plan.vecs // 2):
                to_chip = to_chip + jnp.where(chip == k, k ^ dy, 0)
        first = pl.multiple_of((2 * to_chip + core) * plan.columns, plan.columns)
        for r in range(plan.own):
            out[0, r] = y[to_x * plan.own + r, pl.ds(first, plan.columns), :]
            out[1, r] = got_core[to_x * (plan.vecs // 2) + to_chip, r]


def leave(plan, y, got_core):
    n = len(chip_order(plan))
    return call(
        functools.partial(leave_kernel, plan), (exit_shape(plan, 2),) * n, vm(2), (y, got_core), moved=4 << 20
    )


def arrive_kernel(plan, *refs):
    *gots, out = refs
    x, z, v, s = place(plan)
    core, chip = lax.rem(v, 2), lax.div(v, 2)
    for (dx, dy), got in zip(chip_order(plan), gots, strict=True):
        for other in range(2):
            seg = jnp.int32(0)
            for m in range(2):
                for at in range(plan.vecs):
                    source = plan.seg[m ^ dx, (at ^ other) ^ (2 * dy)]
                    seg = seg + jnp.where((x == m) & (v == at), source, 0)
            for r in range(plan.own):
                for p in range(plan.run):
                    to = pl.multiple_of((r * SPAN + column(plan, seg, p)) * plan.width, plan.width)
                    out[:, pl.ds(to, plan.width)] = got[other, r, :, p * plan.width : (p + 1) * plan.width]


def arrive(plan, gots):
    return call(
        functools.partial(arrive_kernel, plan),
        shape(plan.columns, plan.blocks * plan.width),
        vm(len(gots)),
        tuple(gots),
        moved=2 << 20,
    )


def gram_pieces(plan):
    rows = plan.vectors // plan.meshes
    height = 8 if rows % 8 == 0 else rows
    return rows, height, rows // height


def image_kernel(plan, part, u, w_out, scale, got_a, got_b, got_core, got_ring, y, mass, out, *halos):
    row, _, _ = halo_terms(plan, u, w_out, got_a, got_b, got_core, got_ring, *halos)
    stiff = jnp.zeros((plan.vectors, plan.vectors), F32)
    for i in range(plan.rows):
        values = finished_row(plan, i, part, scale, 1.0, row(i))
        image = jnp.concatenate([value.astype(BF16) for value in values], axis=1)
        stiff += dot_turned(image, y[i].astype(BF16))
    rows, height, count = gram_pieces(plan)
    both = (stiff, mass[...])
    for m in range(plan.meshes):
        for v in range(plan.vecs):
            lanes = slice(v * plan.columns, (v + 1) * plan.columns)
            out[m * plan.vecs + v] = jnp.concatenate(
                [g[m * rows + h * height : m * rows + (h + 1) * height, lanes] for g in both for h in range(count)],
                axis=1,
            )


def image(plan, part, u, w_out, scale, got, y, mass):
    rows, height, count = gram_pieces(plan)
    args = (part, u, w_out, scale) + tuple(got) + (y, mass)
    return call(
        functools.partial(image_kernel, plan),
        shape(plan.meshes * plan.vecs, height, 2 * count * plan.columns),
        vm(len(args)),
        args,
        halo_scratch(plan),
        flops=50 << 20,
        moved=5 << 20,
    )


def sum_kernel(plan, got, stiff, mass):
    rows, height, count = gram_pieces(plan)
    total = jnp.sum(got[...], axis=0)
    for k, out in enumerate((stiff, mass)):
        for h in range(count):
            lo = (k * count + h) * plan.columns
            out[h * height : (h + 1) * height, :] = total[:, lo : lo + plan.columns]


def shards(plan, panel, orient, mass, diag, near, far):
    w = plan.width
    panel = panel.T
    orient, mass = orient.reshape(plan.blocks, w), mass.reshape(plan.blocks, w)
    scale_own, chunks, own, first, rest = prepare(plan, panel, orient, mass, diag, near, far)

    def half(m, v):
        return m ^ 1, v

    first = plan.swap(first, half)
    rest = plan.swap(rest, half)
    groups = [
        [(2 * z + d // plan.vecs) * plan.vecs + d % plan.vecs for d in range(plan.segments)] for z in range(plan.layers)
    ]
    got = lax.all_to_all(chunks, BOTH, 0, 0, tiled=True, axis_index_groups=groups)
    above = jnp.where(lax.axis_index("mesh") % 2 == 0, own, first[: plan.run + 1])
    pairs = [(m * plan.vecs + v, (m - 2) * plan.vecs + v) for m in range(2, plan.meshes) for v in range(plan.vecs)]
    below = lax.ppermute(above, BOTH, pairs)

    y, scale, *field = begin(plan, got, scale_own, first)
    w_in, w_out = weights(plan, diag, near, far, first, rest, below)

    def exchange(field):
        u, a, b, core, ring = field
        return u, (
            plan.swap(a, plan.layer_a),
            plan.swap(b, plan.layer_b),
            plan.swap(core, plan.core_swap),
            plan.swap(ring, plan.ring_swap),
        )

    for application in range(APPS):
        before = None
        for step in range(DEGREE):
            factors = (2.0 / RADIUS, -2.0 * CENTER / RADIUS, -1.0) if step else (1.0 / RADIUS, -CENTER / RADIUS, 0.0)
            u, halos = exchange(field)
            (part,) = inner(plan, factors, u, y, before, w_in, scale)
            leaving = application == APPS - 1 and step == DEGREE - 1
            new, *field = outer(plan, factors[0], part, u, w_out, scale, halos, leaving)
            before, y = y, new
    *field, exit_core = field
    u, halos = exchange(field)
    part, mass_gram = inner(plan, (1.0, 0.0, 0.0), u, y, None, w_in, scale, gram=True)
    got_core = plan.swap(exit_core, plan.core_swap)
    parts = leave(plan, y, got_core)
    kept = []
    for (dx, dy), sent in zip(chip_order(plan), parts, strict=True):
        if dx or dy:
            sent = plan.swap(sent, lambda m, v, dx=dx, dy=dy: (m ^ dx, v ^ (2 * dy)))
        kept.append(sent)
    grams = image(plan, part, u, w_out, scale, halos, y, mass_gram)
    grams = lax.all_to_all(grams, BOTH, 0, 0, tiled=True)
    rows = gram_pieces(plan)[0]
    stiff_gram, mass_gram = call(
        functools.partial(sum_kernel, plan), (shape(rows, plan.columns),) * 2, vm(1), (grams,), moved=1 << 17
    )
    filtered = arrive(plan, kept)
    return filtered.T, stiff_gram.T, mass_gram.T


def solution(mesh):
    placed = (P("mesh", "vec"), P("mesh"), P("mesh"), P("mesh"), P("mesh"), P("mesh"))

    def run(panel, orient, mass, diag, near, far):
        meshes, vecs = mesh.shape["mesh"], mesh.shape["vec"]
        plan = Plan(meshes, vecs, diag.shape[0] // meshes, diag.shape[1], panel.shape[1] // vecs)
        return jax.shard_map(
            functools.partial(shards, plan),
            mesh=mesh,
            in_specs=placed,
            out_specs=(P("mesh", "vec"), P("vec", "mesh"), P("vec", "mesh")),
            check_vma=False,
        )(panel, orient, mass, diag, near, far)

    return run
```

```python
import functools

import jax
import jax.numpy as jnp
from jax import lax
from jax.experimental import pallas as pl
from jax.experimental.pallas import tpu as pltpu
from jax.sharding import PartitionSpec as P

SPAN = 32
DEGREE = 4
APPS = 2
CENTER = 6.0
RADIUS = 8.0

BOTH = ("mesh", "vec")
ORDER = ("ring", "a", "b", "core")
F32 = jnp.float32
BF16 = jnp.bfloat16
VMEM_LIMIT = 24 * 1024 * 1024


def gray(t):
    return t ^ (t >> 1)


class Plan:
    def __init__(self, meshes, vecs, blocks, width, columns):
        self.meshes, self.vecs, self.blocks, self.width, self.columns = meshes, vecs, blocks, width, columns
        self.ring = [(0, gray(t)) for t in range(vecs)] + [(1, gray(t)) for t in reversed(range(vecs))]
        self.segments = 2 * vecs
        self.seg = {place: s for s, place in enumerate(self.ring)}
        self.layers = meshes // 2
        self.own = blocks // SPAN
        self.rows = 2 * self.own
        self.run = SPAN // self.segments
        self.half = self.run // 2
        self.lanes = self.run * width
        self.vectors = vecs * columns
        self.inner, self.outer = {}, {}
        for i in range(self.rows):
            for p in range(self.run):
                self.inner["D", i, p] = len(self.inner)
        for i in range(self.rows):
            for p in range(1, self.run):
                self.inner["N", i, p] = len(self.inner)
        for i in range(1, self.rows):
            for p in range(self.run):
                self.inner["F", i, p] = len(self.inner)
        for p in range(self.run):
            self.outer["F", 0, p] = len(self.outer)
        for p in range(self.run):
            self.outer["F", self.rows, p] = len(self.outer)
        for i in range(self.rows):
            self.outer["N", i, 0] = len(self.outer)
            self.outer["N", i, self.run] = len(self.outer)
        for i in (0, self.rows - 1, self.rows):
            self.outer["N", i, self.half] = len(self.outer)
        self.count = self.own * self.run
        self.aux = self.run + 1
        self.n_first = self.aux + 1 + self.count // 2
        self.n_rest = self.own * (self.run + 1) - 1 + (self.own - 1) * self.run

    def received(self, kind, r, p):
        if kind == "N":
            if r == 0 and p == self.half:
                return 0, self.run
            return 1, r * (self.run + 1) + p - (r > 0 or p > self.half)
        if r == 0:
            return 0, p
        return 1, self.own * (self.run + 1) - 1 + (r - 1) * self.run + p

    def swap(self, x, partner):
        pairs = []
        for m in range(self.meshes):
            for v in range(self.vecs):
                to, at = partner(m, v)
                pairs.append((m * self.vecs + v, to * self.vecs + at))
        return lax.ppermute(x, BOTH, pairs)

    def layer_a(self, m, v):
        to = m ^ 2
        return (to, v) if to < self.meshes else (m, v ^ 1)

    def layer_b(self, m, v):
        z = m // 2
        to = m + 2 if z % 2 else m - 2
        return (to, v) if 0 <= to < self.meshes else (m, v ^ 1)

    def ring_swap(self, m, v):
        s = self.seg[m % 2, v]
        x, at = self.ring[(s + 1) % self.segments if s % 2 else (s - 1) % self.segments]
        return m - m % 2 + x, at

    def core_swap(self, m, v):
        return m, v ^ 1


def place(plan):
    m, v = lax.axis_index("mesh"), lax.axis_index("vec")
    x, z = lax.rem(m, 2), lax.div(m, 2)
    s = jnp.int32(0)
    for k, (a, b) in enumerate(plan.ring):
        s = s + jnp.where((x == a) & (v == b), k, 0)
    return x, z, v, s


def column(plan, s, p):
    return lax.rem(plan.run * s + (p - plan.half + SPAN), SPAN)


def pieces(plan, s):
    found = []
    for p in range(plan.run):
        j = (plan.run * s + p - plan.half) % SPAN
        if found and found[-1][1] + found[-1][2] == j:
            found[-1][2] += 1
        else:
            found.append([p, j, 1])
    return found


def dot(u, w):
    return lax.dot_general(u, w, (((1,), (0,)), ((), ())), preferred_element_type=F32)


def dot_turned(u, w):
    return lax.dot_general(u, w, (((1,), (1,)), ((), ())), preferred_element_type=F32)


def call(name, kernel, outs, ins, args, scratch=(), flops=0, moved=0):
    return pl.pallas_call(
        kernel,
        name=name,
        out_shape=outs,
        in_specs=ins,
        out_specs=jax.tree.map(lambda _: pl.BlockSpec(memory_space=pltpu.VMEM), outs),
        scratch_shapes=list(scratch),
        compiler_params=pltpu.CompilerParams(vmem_limit_bytes=VMEM_LIMIT),
        cost_estimate=pl.CostEstimate(flops=flops, bytes_accessed=moved, transcendentals=0),
    )(*args)


def vm(n):
    return [pl.BlockSpec(memory_space=pltpu.VMEM)] * n


def in_hbm(n):
    return [pl.BlockSpec(memory_space=pltpu.HBM)] * n


def shape(*dims, dtype=F32):
    return jax.ShapeDtypeStruct(dims, dtype)


class Copies:
    def __init__(self, sems):
        self.sems, self.started = sems, []

    def start(self, src, dst):
        copy = pltpu.make_async_copy(src, dst, self.sems.at[len(self.started)])
        copy.start()
        self.started.append(copy)

    def start_one(self, first, src, dst, otherwise):
        sem = self.sems.at[len(self.started)]

        @pl.when(first)
        def _():
            pltpu.make_async_copy(src, dst, sem).start()

        @pl.when(jnp.logical_not(first))
        def _():
            pltpu.make_async_copy(src, otherwise, sem).start()

        self.started.append(pltpu.make_async_copy(src, dst, sem))

    def wait(self, lo=0, hi=None):
        for copy in self.started[lo:hi]:
            copy.wait()


def block_of(plan, src, seg, r, p):
    return src.at[r * SPAN + column(plan, seg, p)]


def upper(w):
    return lax.broadcasted_iota(jnp.int32, (w, w), 0) <= lax.broadcasted_iota(jnp.int32, (w, w), 1)


def on_diagonal(w):
    return lax.broadcasted_iota(jnp.int32, (w, w), 0) == lax.broadcasted_iota(jnp.int32, (w, w), 1)


def prepare_kernel(plan, panel, orient, mass, diag, near, far, scale, enter, own_enter, first, *scratch):
    signs, masses, blocks, parts, sems = scratch
    x, z, v, s = place(plan)
    other = plan.segments - 1 - s
    core = lax.rem(v, 2)
    copies = Copies(sems)
    copies.start(orient, signs)
    copies.start(mass, masses)
    for r in range(plan.own):
        for p in range(plan.run):
            copies.start(block_of(plan, diag, other, r, p), blocks.at[r * plan.run + p])
    for d in range(plan.segments):
        chip, at_core = divmod(d, 2)
        seg = plan.seg[d // plan.vecs, d % plan.vecs]
        for r in range(plan.own):
            for p, j, n in pieces(plan, seg):
                src = panel.at[:, pl.ds((r * SPAN + j) * plan.width, n * plan.width)]
                lanes = pl.ds(p * plan.width, n * plan.width)
                copies.start_one(core == at_core, src, own_enter.at[chip, r, :, lanes], enter.at[chip, r, :, lanes])
    for p in range(plan.run):
        copies.start(block_of(plan, far, other, 0, p), first.at[p])
    copies.start(block_of(plan, near, other, 0, plan.half), first.at[plan.run])
    copies.wait(0, 2)
    scale[...] = signs[...].astype(F32) * lax.rsqrt(masses[...])
    parts[...] = jnp.zeros_like(parts)
    for r in range(plan.own):
        for p in range(plan.run):
            value = scale[pl.ds(r * SPAN + column(plan, other, p), 1), :]
            for part in range(3):
                rounded = value.astype(BF16).astype(F32)
                at = part * plan.count + r * plan.run + p
                parts[at : at + 1, :] = rounded
                value = value - rounded
    copies.wait(2, 2 + plan.count)
    keep, line = upper(plan.width), on_diagonal(plan.width)
    for k in range(plan.count // 2):
        one, two = blocks[2 * k].astype(F32), blocks[2 * k + 1].astype(F32)
        first[plan.aux + 1 + k] = jnp.where(keep, one, two).astype(BF16)
        at = 3 * plan.count + k
        parts[at : at + 1, :] = jnp.sum(jnp.where(line, two, 0.0), axis=0, keepdims=True)
    first[plan.aux] = parts[...].astype(BF16)
    copies.wait(2 + plan.count)


def prepare(plan, panel, orient, mass, diag, near, far):
    w = plan.width
    n_copies = 2 + plan.count + plan.run + 1
    n_copies += plan.own * sum(len(pieces(plan, seg)) for seg in range(plan.segments))
    args = [pltpu.with_memory_space_constraint(a, pltpu.HBM) for a in (panel, orient, mass, diag, near, far)]
    entering = shape(plan.segments // 2, plan.own, plan.columns, plan.lanes)
    return call(
        "prepare",
        functools.partial(prepare_kernel, plan),
        (shape(plan.blocks, w), entering, entering, shape(plan.n_first, w, w, dtype=BF16)),
        in_hbm(6),
        args,
        [
            pltpu.VMEM((plan.blocks, w), orient.dtype),
            pltpu.VMEM((plan.blocks, w), F32),
            pltpu.VMEM((plan.count, w, w), BF16),
            pltpu.VMEM((w, w), F32),
            pltpu.SemaphoreType.DMA((n_copies,)),
        ],
        moved=4 << 20,
    )


def fetch_kernel(plan, diag, near, far, own_diag, own_first, own_rest, rest, sems):
    x, z, v, s = place(plan)
    copies = Copies(sems)
    for seg, heads, tail in ((plan.segments - 1 - s, None, rest), (s, own_first, own_rest)):
        for kind, src in (("N", near), ("F", far)):
            for r in range(plan.own):
                for p in range(plan.run + (kind == "N")):
                    which, at = plan.received(kind, r, p)
                    if which == 1:
                        copies.start(block_of(plan, src, seg, r, p), tail.at[at])
                    elif heads is not None:
                        copies.start(block_of(plan, src, seg, r, p), heads.at[at])
    for r in range(plan.own):
        for p in range(plan.run):
            copies.start(block_of(plan, diag, s, r, p), own_diag.at[r * plan.run + p])
    copies.wait()


def fetch(plan, diag, near, far):
    w = plan.width
    args = [pltpu.with_memory_space_constraint(a, pltpu.HBM) for a in (diag, near, far)]
    return call(
        "fetch",
        functools.partial(fetch_kernel, plan),
        tuple(shape(n, w, w, dtype=BF16) for n in (plan.count, plan.run + 1, plan.n_rest, plan.n_rest)),
        in_hbm(3),
        args,
        [pltpu.SemaphoreType.DMA((2 * plan.n_rest + plan.run + 1 + plan.count,))],
        moved=3 << 20,
    )


def enter_kernel(plan, own_enter, got_core, *outs):
    x, z, v, s = place(plan)
    core, chip = lax.rem(v, 2), lax.div(v, 2)
    for (dx, dy), out in zip(chip_order(plan), outs, strict=True):
        at = chip_at(plan, x, chip, dx, dy)
        for r in range(plan.own):
            out[core, r] = own_enter[at, r]
            out[1 - core, r] = got_core[at, r]


def enter(plan, own_enter, got_core):
    n = len(chip_order(plan))
    return call(
        "enter",
        functools.partial(enter_kernel, plan),
        (exit_shape(plan, 2),) * n,
        vm(2),
        (own_enter, got_core),
        moved=4 << 20,
    )


def chip_order(plan):
    pairs = [(dx, dy) for dx in range(2) for dy in range(plan.vecs // 2)]
    return pairs[plan.vecs // 2 :] + pairs[: plan.vecs // 2]


def chip_at(plan, x, chip, dx, dy):
    to_x = 1 - x if dx else x
    to_chip = chip
    if dy:
        to_chip = jnp.int32(0)
        for k in range(plan.vecs // 2):
            to_chip = to_chip + jnp.where(chip == k, k ^ dy, 0)
    return to_x * (plan.vecs // 2) + to_chip


def emit(plan, u_out, send_a, send_b, send_core, send_ring):
    x, z, v, s = place(plan)
    last, width = plan.rows - 1, plan.width
    even_layer, even_seg = lax.rem(z, 2) == 0, lax.rem(s, 2) == 0
    send_a[...] = lax.select(even_layer, u_out[last], u_out[0])
    send_b[...] = lax.select(even_layer, u_out[0], u_out[last])
    for i in range(plan.rows):
        left, right = u_out[i, :, :width], u_out[i, :, plan.lanes - width :]
        send_core[i] = lax.select(even_seg, right, left)
        send_ring[i] = lax.select(even_seg, left, right)


def sends(plan):
    w = plan.width
    edge = shape(plan.vectors, plan.lanes, dtype=BF16)
    side = shape(plan.rows, plan.vectors, w, dtype=BF16)
    return (shape(plan.rows, plan.vectors, plan.lanes, dtype=BF16), edge, edge, side, side)


def begin_kernel(plan, scale_own, first, *refs):
    gots, refs = refs[: plan.vecs], refs[plan.vecs :]
    y_out, scale_out, u_out, send_a, send_b, send_core, send_ring = refs
    x, z, v, s = place(plan)
    count = plan.count
    parts = first[plan.aux].astype(F32)
    theirs = (parts[:count] + parts[count : 2 * count]) + parts[2 * count : 3 * count]
    chip = lax.div(v, 2)
    for (dx, dy), got in zip(chip_order(plan), gots, strict=True):
        from_x = 1 - x if dx else x
        from_chip = chip_at(plan, x, chip, dx, dy) - from_x * (plan.vecs // 2)
        for core in range(2):
            lo = pl.multiple_of((2 * from_chip + core) * plan.columns, plan.columns)
            for r in range(plan.own):
                y_out[from_x * plan.own + r, pl.ds(lo, plan.columns), :] = got[core, r]
    for i in range(plan.rows):
        half, r = divmod(i, plan.own)
        for p in range(plan.run):
            mine = scale_own[pl.ds(r * SPAN + column(plan, s, p), 1), :]
            scale_out[pl.ds(i * plan.run + p, 1), :] = jnp.where(
                x == half, mine, theirs[r * plan.run + p : r * plan.run + p + 1]
            )
    for i in range(plan.rows):
        for p in range(plan.run):
            row, lanes = scale_out[pl.ds(i * plan.run + p, 1), :], slice(p * plan.width, (p + 1) * plan.width)
            u_out[i, :, lanes] = (row * y_out[i, :, lanes]).astype(BF16)
    emit(plan, u_out, send_a, send_b, send_core, send_ring)


def begin(plan, gots, scale_own, first):
    return call(
        "begin", functools.partial(begin_kernel, plan),
        (shape(plan.rows, plan.vectors, plan.lanes), shape(plan.rows * plan.run, plan.width)) + sends(plan),
        vm(2 + len(gots)),
        (scale_own, first, *gots),
        moved=4 << 20,
    )


def weights_kernel(plan, own_diag, own_first, own_rest, first, rest, below, inner, outer):
    x, _, _, _ = place(plan)
    keep, line = upper(plan.width), on_diagonal(plan.width)
    lines = first[plan.aux].astype(F32)
    for k in range(plan.count // 2):
        both = first[plan.aux + 1 + k].astype(F32)
        turned = both.T
        at = 3 * plan.count + k
        found = jnp.where(keep, both, turned), jnp.where(line, lines[at : at + 1], jnp.where(keep, turned, both))
        for at, value in zip((2 * k, 2 * k + 1), found, strict=True):
            r, p = divmod(at, plan.run)
            value = value.astype(BF16)
            for half in range(2):
                mine, theirs = plan.inner["D", half * plan.own + r, p], plan.inner["D", (1 - half) * plan.own + r, p]

                @pl.when(x == half)
                def _():
                    inner[mine] = own_diag[at]
                    inner[theirs] = value

    for half in range(2):

        @pl.when(x == half)
        def _():
            for table, out in ((plan.inner, inner), (plan.outer, outer)):
                for (kind, i, p), k in table.items():
                    if i == plan.rows:
                        out[k] = below[p if kind == "F" else plan.run]
                    elif kind != "D":
                        group, r = divmod(i, plan.own)
                        which, index = plan.received(kind, r, p)
                        source = (own_first, own_rest) if group == half else (first, rest)
                        out[k] = source[which][index]


def weights(plan, own_diag, own_first, own_rest, first, rest, below):
    w = plan.width
    return call(
        "weights",
        functools.partial(weights_kernel, plan),
        (shape(len(plan.inner), w, w, dtype=BF16), shape(len(plan.outer), w, w, dtype=BF16)),
        vm(6),
        (own_diag, own_first, own_rest, first, rest, below),
        moved=4 << 20,
    )


def inner_kernel(plan, factors, has_before, gram, *refs):
    a, b, c = factors
    refs = list(refs)
    u, y = refs[:2]
    before = refs[2] if has_before else None
    w_in, scale, part = refs[2 + has_before : 5 + has_before]
    x, z, v, s = place(plan)
    wrap = (s == 0).astype(jnp.int32)
    width, half, last = plan.width, plan.half, plan.rows - 1
    at = plan.inner
    for i in range(plan.rows):
        for p in range(plan.run):
            lanes = slice(p * width, (p + 1) * width)
            total = dot(u[i, :, lanes], w_in[at["D", i, p]])
            if p == half:
                if i > 0:
                    total += dot_turned(u[i - wrap, :, (p - 1) * width : p * width], w_in[at["N", i, p]])
            elif p > 0:
                total += dot_turned(u[i, :, (p - 1) * width : p * width], w_in[at["N", i, p]])
            if p + 1 == half:
                if i < last:
                    near = at["N", i, half] + wrap * (plan.run - 1)
                    total += dot(u[i + wrap, :, (p + 1) * width : (p + 2) * width], w_in[near])
            elif p + 1 < plan.run:
                total += dot(u[i, :, (p + 1) * width : (p + 2) * width], w_in[at["N", i, p + 1]])
            if i > 0:
                total += dot_turned(u[i - 1, :, lanes], w_in[at["F", i, p]])
            if i < last:
                total += dot(u[i + 1, :, lanes], w_in[at["F", i + 1, p]])
            result = (a * scale[pl.ds(i * plan.run + p, 1), :]) * total
            if b:
                result += b * y[i, :, lanes]
            if has_before:
                result += c * before[i, :, lanes]
            part[i, :, lanes] = result
    if gram:
        mass = refs[5 + has_before]
        total = jnp.zeros(mass.shape, F32)
        for i in range(plan.rows):
            rounded = y[i].astype(BF16)
            total += dot_turned(rounded, rounded)
        mass[...] = total


def inner(plan, factors, u, y, before, w_in, scale, gram=False):
    has_before = before is not None
    args = (u, y) + ((before,) if has_before else ()) + (w_in, scale)
    outs = (shape(plan.rows, plan.vectors, plan.lanes),)
    if gram:
        outs += (shape(plan.vectors, plan.vectors),)
    return call(
        "inner", functools.partial(inner_kernel, plan, factors, has_before, gram),
        outs,
        vm(len(args)),
        args,
        flops=130 << 20,
        moved=5 << 20,
    )


def halo_terms(plan, u, w_out, *gots):
    x, z, v, s = place(plan)
    even_layer, even_seg, wrap = lax.rem(z, 2) == 0, lax.rem(s, 2) == 0, s == 0
    width, half, last, at = plan.width, plan.half, plan.rows - 1, plan.outer
    got = dict(zip(ORDER, gots, strict=True))
    got_a, got_b, got_ring, got_core = got["a"], got["b"], got["ring"], got["core"]
    none = jnp.zeros(got_a.shape, BF16)
    top = lax.select(z == 0, none, lax.select(even_layer, got_b[...], got_a[...]))
    bottom = lax.select(z == plan.layers - 1, none, lax.select(even_layer, got_a[...], got_b[...]))
    left = [lax.select(even_seg, got_ring[i], got_core[i]) for i in range(plan.rows)]
    right = [lax.select(even_seg, got_core[i], got_ring[i]) for i in range(plan.rows)]

    def row(i):
        found = {0: dot_turned(left[i], w_out[at["N", i, 0]])}
        found[plan.run - 1] = dot(right[i], w_out[at["N", i, plan.run]])

        def add(p, term):
            found[p] = found[p] + term if p in found else term

        if i == 0:
            for p in range(plan.run):
                add(p, dot_turned(top[:, p * width : (p + 1) * width], w_out[at["F", 0, p]]))
            lanes = slice((half - 1) * width, half * width)
            before = lax.select(wrap, top[:, lanes], u[0, :, lanes])
            add(half, dot_turned(before, w_out[at["N", 0, half]]))
        if i == last:
            for p in range(plan.run):
                add(p, dot(bottom[:, p * width : (p + 1) * width], w_out[at["F", plan.rows, p]]))
            lanes = slice(half * width, (half + 1) * width)
            after = lax.select(wrap, bottom[:, lanes], u[last, :, lanes])
            here, there = at["N", last, half], at["N", plan.rows, half]
            add(half - 1, dot(after, w_out[here + wrap.astype(jnp.int32) * (there - here)]))
        return found

    return row


def finished_row(plan, i, part, scale, factor, terms):
    out = []
    for p in range(plan.run):
        value = part[i, :, p * plan.width : (p + 1) * plan.width]
        if p in terms:
            value += (factor * scale[pl.ds(i * plan.run + p, 1), :]) * terms[p]
        out.append(value)
    return out


def outer_kernel(plan, factor, leaving, part, u, w_out, scale, got_0, got_1, got_2, got_3, *refs):
    refs = list(refs)
    y_out, u_out, send_a, send_b, send_core, send_ring = refs[:6]
    row = halo_terms(plan, u, w_out, got_0, got_1, got_2, got_3)
    width = plan.width
    for i in range(plan.rows):
        values = finished_row(plan, i, part, scale, factor, row(i))
        for p, value in enumerate(values):
            y_out[i, :, p * width : (p + 1) * width] = value
            u_out[i, :, p * width : (p + 1) * width] = (scale[pl.ds(i * plan.run + p, 1), :] * value).astype(BF16)
    emit(plan, u_out, send_a, send_b, send_core, send_ring)
    if leaving:
        exit_core = refs[6]
        core = lax.rem(lax.axis_index("vec"), 2)
        for k in range(plan.segments // 2):
            half, chip = divmod(k, plan.vecs // 2)
            first = pl.multiple_of((2 * chip + 1 - core) * plan.columns, plan.columns)
            for r in range(plan.own):
                exit_core[k, r] = y_out[half * plan.own + r, pl.ds(first, plan.columns), :]


def exit_shape(plan, n):
    return shape(n, plan.own, plan.columns, plan.lanes)


def outer(plan, factor, part, u, w_out, scale, got, leaving=False):
    outs = (shape(plan.rows, plan.vectors, plan.lanes),) + sends(plan)
    if leaving:
        outs += (exit_shape(plan, plan.segments // 2),)
    args = (part, u, w_out, scale) + tuple(got)
    return call(
        "outer", functools.partial(outer_kernel, plan, factor, leaving),
        outs,
        vm(len(args)),
        args,
        flops=40 << 20,
        moved=5 << 20,
    )


def leave_kernel(plan, y, got_core, *outs):
    x, z, v, s = place(plan)
    core, chip = lax.rem(v, 2), lax.div(v, 2)
    for (dx, dy), out in zip(chip_order(plan), outs, strict=True):
        at = chip_at(plan, x, chip, dx, dy)
        to_x = 1 - x if dx else x
        first = pl.multiple_of((2 * (at - to_x * (plan.vecs // 2)) + core) * plan.columns, plan.columns)
        for r in range(plan.own):
            out[0, r] = y[to_x * plan.own + r, pl.ds(first, plan.columns), :]
            out[1, r] = got_core[at, r]


def leave(plan, y, got_core):
    n = len(chip_order(plan))
    return call(
        "leave", functools.partial(leave_kernel, plan), (exit_shape(plan, 2),) * n, vm(2), (y, got_core), moved=4 << 20
    )


def arrive_kernel(plan, *refs):
    *gots, out = refs
    x, z, v, s = place(plan)
    core, chip = lax.rem(v, 2), lax.div(v, 2)
    for (dx, dy), got in zip(chip_order(plan), gots, strict=True):
        for other in range(2):
            seg = jnp.int32(0)
            for m in range(2):
                for at in range(plan.vecs):
                    source = plan.seg[m ^ dx, (at ^ other) ^ (2 * dy)]
                    seg = seg + jnp.where((x == m) & (v == at), source, 0)
            for r in range(plan.own):
                for p in range(plan.run):
                    to = pl.multiple_of((r * SPAN + column(plan, seg, p)) * plan.width, plan.width)
                    out[:, pl.ds(to, plan.width)] = got[other, r, :, p * plan.width : (p + 1) * plan.width]


def arrive(plan, gots):
    return call(
        "arrive", functools.partial(arrive_kernel, plan),
        shape(plan.columns, plan.blocks * plan.width),
        vm(len(gots)),
        tuple(gots),
        moved=2 << 20,
    )


def gram_pieces(plan):
    rows = plan.vectors // plan.meshes
    height = 8 if rows % 8 == 0 else rows
    return rows, height, rows // height


def image_kernel(plan, part, u, w_out, scale, got_0, got_1, got_2, got_3, y, mass, out):
    row = halo_terms(plan, u, w_out, got_0, got_1, got_2, got_3)
    stiff = jnp.zeros((plan.vectors, plan.vectors), F32)
    for i in range(plan.rows):
        values = finished_row(plan, i, part, scale, 1.0, row(i))
        image = jnp.concatenate([value.astype(BF16) for value in values], axis=1)
        stiff += dot_turned(image, y[i].astype(BF16))
    rows, height, count = gram_pieces(plan)
    both = (stiff, mass[...])
    for m in range(plan.meshes):
        for v in range(plan.vecs):
            lanes = slice(v * plan.columns, (v + 1) * plan.columns)
            out[m * plan.vecs + v] = jnp.concatenate(
                [g[m * rows + h * height : m * rows + (h + 1) * height, lanes] for g in both for h in range(count)],
                axis=1,
            )


def image(plan, part, u, w_out, scale, got, y, mass):
    rows, height, count = gram_pieces(plan)
    args = (part, u, w_out, scale) + tuple(got) + (y, mass)
    return call(
        "image", functools.partial(image_kernel, plan),
        shape(plan.meshes * plan.vecs, height, 2 * count * plan.columns),
        vm(len(args)),
        args,
        flops=50 << 20,
        moved=5 << 20,
    )


def sum_kernel(plan, got, stiff, mass):
    rows, height, count = gram_pieces(plan)
    total = jnp.sum(got[...], axis=0)
    for k, out in enumerate((stiff, mass)):
        for h in range(count):
            lo = (k * count + h) * plan.columns
            out[h * height : (h + 1) * height, :] = total[:, lo : lo + plan.columns]


def shards(plan, panel, orient, mass, diag, near, far):
    w = plan.width
    panel = panel.T
    orient, mass = orient.reshape(plan.blocks, w), mass.reshape(plan.blocks, w)
    scale_own, entering, own_entering, first = prepare(plan, panel, orient, mass, diag, near, far)
    own_diag, own_first, own_rest, rest = fetch(plan, diag, near, far)

    def half(m, v):
        return m ^ 1, v

    def spread(parts):
        found = []
        for (dx, dy), sent in zip(chip_order(plan), parts, strict=True):
            if dx or dy:
                sent = plan.swap(sent, lambda m, v, dx=dx, dy=dy: (m ^ dx, v ^ (2 * dy)))
            found.append(sent)
        return found

    first = plan.swap(first, half)
    parts = enter(plan, own_entering, plan.swap(entering, plan.core_swap))
    gots = spread(parts)
    first, rest, *gots = lax.optimization_barrier((first, rest, *gots))
    rest = plan.swap(rest, half)
    above = jnp.where(lax.axis_index("mesh") % 2 == 0, own_first, first[: plan.run + 1])
    pairs = [(m * plan.vecs + v, (m - 2) * plan.vecs + v) for m in range(2, plan.meshes) for v in range(plan.vecs)]
    below = lax.ppermute(above, BOTH, pairs)

    y, scale, *field = begin(plan, gots, scale_own, first)
    w_in, w_out = weights(plan, own_diag, own_first, own_rest, first, rest, below)

    def exchange(field):
        u, a, b, core, ring = field
        got = {
            "a": lambda: plan.swap(a, plan.layer_a),
            "b": lambda: plan.swap(b, plan.layer_b),
            "ring": lambda: plan.swap(ring, plan.ring_swap),
            "core": lambda: plan.swap(core, plan.core_swap),
        }
        return u, tuple(got[name]() for name in ORDER)

    for application in range(APPS):
        before = None
        for step in range(DEGREE):
            factors = (2.0 / RADIUS, -2.0 * CENTER / RADIUS, -1.0) if step else (1.0 / RADIUS, -CENTER / RADIUS, 0.0)
            u, halos = exchange(field)
            (part,) = inner(plan, factors, u, y, before, w_in, scale)
            leaving = application == APPS - 1 and step == DEGREE - 1
            new, *field = outer(plan, factors[0], part, u, w_out, scale, halos, leaving)
            before, y = y, new
    *field, exit_core = field
    u, halos = exchange(field)
    part, mass_gram = inner(plan, (1.0, 0.0, 0.0), u, y, None, w_in, scale, gram=True)
    got_core = plan.swap(exit_core, plan.core_swap)
    part, got_core = lax.optimization_barrier((part, got_core))
    kept = spread(leave(plan, y, got_core))
    grams = image(plan, part, u, w_out, scale, halos, y, mass_gram)
    grams = lax.all_to_all(grams, BOTH, 0, 0, tiled=True)
    rows = gram_pieces(plan)[0]
    stiff_gram, mass_gram = call(
        "sum", functools.partial(sum_kernel, plan), (shape(rows, plan.columns),) * 2, vm(1), (grams,), moved=1 << 17
    )
    filtered = arrive(plan, kept)
    return filtered.T, stiff_gram.T, mass_gram.T


def solution(mesh):
    placed = (P("mesh", "vec"), P("mesh"), P("mesh"), P("mesh"), P("mesh"), P("mesh"))

    def run(panel, orient, mass, diag, near, far):
        meshes, vecs = mesh.shape["mesh"], mesh.shape["vec"]
        plan = Plan(meshes, vecs, diag.shape[0] // meshes, diag.shape[1], panel.shape[1] // vecs)
        return jax.shard_map(
            functools.partial(shards, plan),
            mesh=mesh,
            in_specs=placed,
            out_specs=(P("mesh", "vec"), P("vec", "mesh"), P("vec", "mesh")),
            check_vma=False,
        )(panel, orient, mass, diag, near, far)

    return run
```

```python
import functools

import jax
import jax.numpy as jnp
from jax import lax
from jax.experimental import pallas as pl
from jax.experimental.pallas import tpu as pltpu
from jax.sharding import PartitionSpec as P

SPAN = 32
DEGREE = 4
APPS = 2
CENTER = 6.0
RADIUS = 8.0

BOTH = ("mesh", "vec")
ORDER = ("ring", "a", "b", "core")
F32 = jnp.float32
BF16 = jnp.bfloat16
VMEM_LIMIT = 24 * 1024 * 1024


def gray(t):
    return t ^ (t >> 1)


class Plan:
    def __init__(self, meshes, vecs, blocks, width, columns):
        self.meshes, self.vecs, self.blocks, self.width, self.columns = meshes, vecs, blocks, width, columns
        self.ring = [(0, gray(t)) for t in range(vecs)] + [(1, gray(t)) for t in reversed(range(vecs))]
        self.segments = 2 * vecs
        self.seg = {place: s for s, place in enumerate(self.ring)}
        self.layers = meshes // 2
        self.own = blocks // SPAN
        self.rows = 2 * self.own
        self.run = SPAN // self.segments
        self.half = self.run // 2
        self.lanes = self.run * width
        self.vectors = vecs * columns
        self.count = self.own * self.run
        self.first, self.rest, self.near = {("N", 0, self.half): 0}, {}, {}
        for p in range(self.run):
            self.first["F", 0, p] = len(self.first)
        for p in range(self.run + 1):
            self.first.setdefault(("N", 0, p), len(self.first))
        for r in range(1, self.own):
            for p in range(self.run + 1):
                self.near["N", r, p] = len(self.near)
            for p in range(self.run):
                self.rest["F", r, p] = len(self.rest)
        self.aux = len(self.first)
        self.n_rest = len(self.rest) + self.count // 2
        self.outer = {}
        for p in range(self.run):
            self.outer["F", 0, p] = len(self.outer)
        for i in range(self.rows):
            self.outer["N", i, 0] = len(self.outer)
            self.outer["N", i, self.run] = len(self.outer)
        for i in (0, self.rows - 1):
            self.outer["N", i, self.half] = len(self.outer)

    def swap(self, x, partner):
        pairs = []
        for m in range(self.meshes):
            for v in range(self.vecs):
                to, at = partner(m, v)
                pairs.append((m * self.vecs + v, to * self.vecs + at))
        return lax.ppermute(x, BOTH, pairs)

    def layer_a(self, m, v):
        to = m ^ 2
        return (to, v) if to < self.meshes else (m, v ^ 1)

    def layer_b(self, m, v):
        z = m // 2
        to = m + 2 if z % 2 else m - 2
        return (to, v) if 0 <= to < self.meshes else (m, v ^ 1)

    def ring_swap(self, m, v):
        s = self.seg[m % 2, v]
        x, at = self.ring[(s + 1) % self.segments if s % 2 else (s - 1) % self.segments]
        return m - m % 2 + x, at

    def core_swap(self, m, v):
        return m, v ^ 1


def place(plan):
    m, v = lax.axis_index("mesh"), lax.axis_index("vec")
    x, z = lax.rem(m, 2), lax.div(m, 2)
    s = jnp.int32(0)
    for k, (a, b) in enumerate(plan.ring):
        s = s + jnp.where((x == a) & (v == b), k, 0)
    return x, z, v, s


def column(plan, s, p):
    return lax.rem(plan.run * s + (p - plan.half + SPAN), SPAN)


def pieces(plan, s):
    found = []
    for p in range(plan.run):
        j = (plan.run * s + p - plan.half) % SPAN
        if found and found[-1][1] + found[-1][2] == j:
            found[-1][2] += 1
        else:
            found.append([p, j, 1])
    return found


def dot(u, w):
    return lax.dot_general(u, w, (((1,), (0,)), ((), ())), preferred_element_type=F32)


def dot_turned(u, w):
    return lax.dot_general(u, w, (((1,), (1,)), ((), ())), preferred_element_type=F32)


def call(name, kernel, outs, ins, args, scratch=(), flops=0, moved=0):
    return pl.pallas_call(
        kernel,
        name=name,
        out_shape=outs,
        in_specs=ins,
        out_specs=jax.tree.map(lambda _: pl.BlockSpec(memory_space=pltpu.VMEM), outs),
        scratch_shapes=list(scratch),
        compiler_params=pltpu.CompilerParams(vmem_limit_bytes=VMEM_LIMIT),
        cost_estimate=pl.CostEstimate(flops=flops, bytes_accessed=moved, transcendentals=0),
    )(*args)


def vm(n):
    return [pl.BlockSpec(memory_space=pltpu.VMEM)] * n


def in_hbm(n):
    return [pl.BlockSpec(memory_space=pltpu.HBM)] * n


def shape(*dims, dtype=F32):
    return jax.ShapeDtypeStruct(dims, dtype)


class Copies:
    def __init__(self, sems):
        self.sems, self.started = sems, []

    def start(self, src, dst):
        copy = pltpu.make_async_copy(src, dst, self.sems.at[len(self.started)])
        copy.start()
        self.started.append(copy)

    def start_one(self, first, src, dst, otherwise):
        sem = self.sems.at[len(self.started)]

        @pl.when(first)
        def _():
            pltpu.make_async_copy(src, dst, sem).start()

        @pl.when(jnp.logical_not(first))
        def _():
            pltpu.make_async_copy(src, otherwise, sem).start()

        self.started.append(pltpu.make_async_copy(src, dst, sem))

    def wait(self, lo=0, hi=None):
        for copy in self.started[lo:hi]:
            copy.wait()


def block_of(plan, src, seg, r, p):
    return src.at[r * SPAN + column(plan, seg, p)]


def upper(w):
    return lax.broadcasted_iota(jnp.int32, (w, w), 0) <= lax.broadcasted_iota(jnp.int32, (w, w), 1)


def on_diagonal(w):
    return lax.broadcasted_iota(jnp.int32, (w, w), 0) == lax.broadcasted_iota(jnp.int32, (w, w), 1)


def prepare_kernel(plan, panel, orient, mass, diag, near, far, scale, enter, own_enter, first, *scratch):
    signs, masses, blocks, parts, sems = scratch
    x, z, v, s = place(plan)
    other = plan.segments - 1 - s
    core = lax.rem(v, 2)
    copies = Copies(sems)
    copies.start(orient, signs)
    copies.start(mass, masses)
    for r in range(plan.own):
        for p in range(1, plan.run, 2):
            copies.start(block_of(plan, diag, other, r, p), blocks.at[(r * plan.run + p) // 2])
    for d in range(plan.segments):
        chip, at_core = divmod(d, 2)
        seg = plan.seg[d // plan.vecs, d % plan.vecs]
        for r in range(plan.own):
            for p, j, n in pieces(plan, seg):
                src = panel.at[:, pl.ds((r * SPAN + j) * plan.width, n * plan.width)]
                lanes = pl.ds(p * plan.width, n * plan.width)
                copies.start_one(core == at_core, src, own_enter.at[chip, r, :, lanes], enter.at[chip, r, :, lanes])
    for (kind, r, p), at in plan.first.items():
        copies.start(block_of(plan, near if kind == "N" else far, other, r, p), first.at[at])
    copies.wait(0, 2)
    scale[...] = signs[...].astype(F32) * lax.rsqrt(masses[...])
    parts[...] = jnp.zeros_like(parts)
    for r in range(plan.own):
        for p in range(plan.run):
            value = scale[pl.ds(r * SPAN + column(plan, other, p), 1), :]
            for part in range(3):
                rounded = value.astype(BF16).astype(F32)
                at = part * plan.count + r * plan.run + p
                parts[at : at + 1, :] = rounded
                value = value - rounded
    copies.wait(2, 2 + plan.count // 2)
    line = on_diagonal(plan.width)
    for k in range(plan.count // 2):
        at = 3 * plan.count + k
        parts[at : at + 1, :] = jnp.sum(jnp.where(line, blocks[k].astype(F32), 0.0), axis=0, keepdims=True)
    first[plan.aux] = parts[...].astype(BF16)
    copies.wait(2 + plan.count // 2)


def prepare(plan, panel, orient, mass, diag, near, far):
    w = plan.width
    n_copies = 2 + plan.count // 2 + len(plan.first)
    n_copies += plan.own * sum(len(pieces(plan, seg)) for seg in range(plan.segments))
    args = [pltpu.with_memory_space_constraint(a, pltpu.HBM) for a in (panel, orient, mass, diag, near, far)]
    entering = shape(plan.segments // 2, plan.own, plan.columns, plan.lanes)
    return call(
        "prepare",
        functools.partial(prepare_kernel, plan),
        (shape(plan.blocks, w), entering, entering, shape(plan.aux + 1, w, w, dtype=BF16)),
        in_hbm(6),
        args,
        [
            pltpu.VMEM((plan.blocks, w), orient.dtype),
            pltpu.VMEM((plan.blocks, w), F32),
            pltpu.VMEM((plan.count // 2, w, w), BF16),
            pltpu.VMEM((w, w), F32),
            pltpu.SemaphoreType.DMA((n_copies,)),
        ],
        moved=3 << 20,
    )


def turned(block):
    return block.astype(F32).T.astype(BF16)


def fetch_kernel(plan, diag, near, far, own_first, own_near, own_rest, others, rest, near_turned, far_turned, blocks, sems):
    x, z, v, s = place(plan)
    other = plan.segments - 1 - s
    copies = Copies(sems)
    for r in range(plan.own):
        for p in range(plan.run):
            copies.start(block_of(plan, diag, other, r, p), blocks.at[r * plan.run + p])
    for src, table, theirs, mine in ((near, plan.near, others, own_near), (far, plan.rest, rest, own_rest)):
        for (_, r, p), at in table.items():
            copies.start(block_of(plan, src, other, r, p), theirs.at[at])
            copies.start(block_of(plan, src, s, r, p), mine.at[at])
    for (kind, r, p), at in plan.first.items():
        copies.start(block_of(plan, near if kind == "N" else far, s, r, p), own_first.at[at])
    for r in range(plan.own):
        for p in range(plan.run):
            copies.start(block_of(plan, diag, s, r, p), own_rest.at[len(plan.rest) + r * plan.run + p])
    copies.wait(0, plan.count)
    keep = upper(plan.width)
    for k in range(plan.count // 2):
        one, two = blocks[2 * k].astype(F32), blocks[2 * k + 1].astype(F32)
        rest[len(plan.rest) + k] = jnp.where(keep, one, two).astype(BF16)
    copies.wait(plan.count)
    for r in range(plan.own):
        for p in range(plan.run):
            n, f = ("N", r, p), ("F", r, p)
            near_turned[r * plan.run + p] = turned(own_near[plan.near[n]] if r else own_first[plan.first[n]])
            far_turned[r * plan.run + p] = turned(own_rest[plan.rest[f]] if r else own_first[plan.first[f]])


def fetch(plan, diag, near, far):
    w = plan.width
    args = [pltpu.with_memory_space_constraint(a, pltpu.HBM) for a in (diag, near, far)]
    n_near, n_own = len(plan.near), len(plan.rest) + plan.count
    return call(
        "fetch",
        functools.partial(fetch_kernel, plan),
        tuple(shape(n, w, w, dtype=BF16) for n in (len(plan.first), n_near, n_own, n_near, plan.n_rest, plan.count, plan.count)),
        in_hbm(3),
        args,
        [
            pltpu.VMEM((plan.count, w, w), BF16),
            pltpu.SemaphoreType.DMA((plan.count + 2 * n_near + len(plan.rest) + len(plan.first) + n_own,)),
        ],
        moved=3 << 20,
    )


def enter_kernel(plan, own_enter, got_core, *outs):
    x, z, v, s = place(plan)
    core, chip = lax.rem(v, 2), lax.div(v, 2)
    for (dx, dy), out in zip(chip_order(plan), outs, strict=True):
        at = chip_at(plan, x, chip, dx, dy)
        for r in range(plan.own):
            out[core, r] = own_enter[at, r]
            out[1 - core, r] = got_core[at, r]


def enter(plan, own_enter, got_core):
    n = len(chip_order(plan))
    return call(
        "enter",
        functools.partial(enter_kernel, plan),
        (exit_shape(plan, 2),) * n,
        vm(2),
        (own_enter, got_core),
        moved=4 << 20,
    )


def chip_order(plan):
    pairs = [(dx, dy) for dx in range(2) for dy in range(plan.vecs // 2)]
    return pairs[plan.vecs // 2 :] + pairs[: plan.vecs // 2]


def chip_at(plan, x, chip, dx, dy):
    to_x = 1 - x if dx else x
    to_chip = chip
    if dy:
        to_chip = jnp.int32(0)
        for k in range(plan.vecs // 2):
            to_chip = to_chip + jnp.where(chip == k, k ^ dy, 0)
    return to_x * (plan.vecs // 2) + to_chip


def emit(plan, u_out, send_a, send_b, send_core, send_ring):
    x, z, v, s = place(plan)
    last, width = plan.rows - 1, plan.width
    even_layer, even_seg = lax.rem(z, 2) == 0, lax.rem(s, 2) == 0
    send_a[...] = lax.select(even_layer, u_out[last], u_out[0])
    send_b[...] = lax.select(even_layer, u_out[0], u_out[last])
    for i in range(plan.rows):
        left, right = u_out[i, :, :width], u_out[i, :, plan.lanes - width :]
        send_core[i] = lax.select(even_seg, right, left)
        send_ring[i] = lax.select(even_seg, left, right)


def sends(plan):
    w = plan.width
    edge = shape(plan.vectors, plan.lanes, dtype=BF16)
    side = shape(plan.rows, plan.vectors, w, dtype=BF16)
    return (shape(plan.rows, plan.vectors, plan.lanes, dtype=BF16), edge, edge, side, side)


def begin_kernel(plan, scale_own, first, *refs):
    gots, refs = refs[: plan.vecs], refs[plan.vecs :]
    y_out, scale_out, u_out, send_a, send_b, send_core, send_ring = refs
    x, z, v, s = place(plan)
    count = plan.count
    parts = first[plan.aux].astype(F32)
    theirs = (parts[:count] + parts[count : 2 * count]) + parts[2 * count : 3 * count]
    chip = lax.div(v, 2)
    for (dx, dy), got in zip(chip_order(plan), gots, strict=True):
        from_x = 1 - x if dx else x
        from_chip = chip_at(plan, x, chip, dx, dy) - from_x * (plan.vecs // 2)
        for core in range(2):
            lo = pl.multiple_of((2 * from_chip + core) * plan.columns, plan.columns)
            for r in range(plan.own):
                y_out[from_x * plan.own + r, pl.ds(lo, plan.columns), :] = got[core, r]
    for i in range(plan.rows):
        half, r = divmod(i, plan.own)
        for p in range(plan.run):
            mine = scale_own[pl.ds(r * SPAN + column(plan, s, p), 1), :]
            scale_out[pl.ds(i * plan.run + p, 1), :] = jnp.where(
                x == half, mine, theirs[r * plan.run + p : r * plan.run + p + 1]
            )
    for i in range(plan.rows):
        for p in range(plan.run):
            row, lanes = scale_out[pl.ds(i * plan.run + p, 1), :], slice(p * plan.width, (p + 1) * plan.width)
            u_out[i, :, lanes] = (row * y_out[i, :, lanes]).astype(BF16)
    emit(plan, u_out, send_a, send_b, send_core, send_ring)


def begin(plan, gots, scale_own, first):
    return call(
        "begin", functools.partial(begin_kernel, plan),
        (shape(plan.rows, plan.vectors, plan.lanes), shape(plan.rows * plan.run, plan.width)) + sends(plan),
        vm(2 + len(gots)),
        (scale_own, first, *gots),
        moved=4 << 20,
    )


def late_kernel(
    plan, own_first, own_near, own_rest, first, others, rest, near_turned, far_turned, pairs, middle, ends, spans, outer
):
    x, _, _, _ = place(plan)
    w, last = plan.width, plan.rows - 1
    keep, line = upper(w), on_diagonal(w)
    diagonals = first[plan.aux].astype(F32)
    theirs = []
    for k in range(plan.count // 2):
        both = rest[len(plan.rest) + k].astype(F32)
        flipped = both.T
        at = 3 * plan.count + k
        theirs.append(jnp.where(keep, both, flipped).astype(BF16))
        theirs.append(jnp.where(line, diagonals[at : at + 1], jnp.where(keep, flipped, both)).astype(BF16))
    lo, hi = slice(0, w), slice(w, 2 * w)
    for half in range(2):

        @pl.when(x == half)
        def _():
            for i in range(plan.rows):
                group, r = divmod(i, plan.own)
                mine = group == half

                def block(kind, p):
                    key = kind, r, p
                    if r == 0:
                        return (own_first if mine else first)[plan.first[key]]
                    if kind == "N":
                        return (own_near if mine else others)[plan.near[key]]
                    return (own_rest if mine else rest)[plan.rest[key]]

                outer[plan.outer["N", i, plan.run]] = block("N", plan.run)
                for p in range(plan.run):
                    at, k, q = i * plan.run + p, (i * plan.run + p) // 2, p % 2
                    own = own_rest[len(plan.rest) + r * plan.run + p] if mine else theirs[r * plan.run + p]
                    pairs[k, (lo, hi)[q], (lo, hi)[q]] = own
                    near = block("N", p)
                    near_flipped = near_turned[r * plan.run + p] if mine else turned(near)
                    if q:
                        pairs[k, lo, hi] = near_flipped
                        pairs[k, hi, lo] = near
                    if p == 0:
                        outer[plan.outer["N", i, 0]] = near_flipped
                    if p == plan.half:
                        spans[i] = near_flipped
                        spans[plan.rows + i] = near
                        if i == 0:
                            outer[plan.outer["N", 0, p]] = near_flipped
                        if i == last:
                            outer[plan.outer["N", last, p]] = near
                    far = block("F", p)
                    far_flipped = far_turned[r * plan.run + p] if mine else turned(far)
                    if i == 0:
                        outer[plan.outer["F", 0, p]] = far_flipped
                    elif i == last:
                        ends[plan.run + p] = far_flipped
                    else:
                        middle[at - plan.run, lo] = far_flipped
                    if i == 1:
                        ends[p] = far
                    elif i > 1:
                        middle[at - 2 * plan.run, hi] = far


def late(plan, *args):
    w = plan.width
    return call(
        "late",
        functools.partial(late_kernel, plan),
        (
            shape(plan.rows * plan.run // 2, 2 * w, 2 * w, dtype=BF16),
            shape((plan.rows - 2) * plan.run, 2 * w, w, dtype=BF16),
            shape(2 * plan.run, w, w, dtype=BF16),
            shape(2 * plan.rows, w, w, dtype=BF16),
            shape(len(plan.outer), w, w, dtype=BF16),
        ),
        vm(len(args)),
        args,
        moved=4 << 20,
    )


def inner_kernel(plan, factors, has_before, gram, u, y, pairs, middle, ends, spans, scale, *refs):
    a, b, c = factors
    before = refs[0] if has_before else None
    part = refs[has_before]
    x, z, v, s = place(plan)
    wrap = (s == 0).astype(jnp.int32)
    width, half, last = plan.width, plan.half, plan.rows - 1
    for i in range(plan.rows):
        for k in range(plan.run // 2):
            two = dot(u[i, :, 2 * k * width : (2 * k + 2) * width], pairs[i * plan.run // 2 + k])
            for p in (2 * k, 2 * k + 1):
                lanes = slice(p * width, (p + 1) * width)
                total = two[:, (p % 2) * width : (p % 2 + 1) * width]
                if i == 0:
                    total += dot(u[1, :, lanes], ends[p])
                elif i == last:
                    total += dot(u[last - 1, :, lanes], ends[plan.run + p])
                else:
                    around = jnp.concatenate([u[i - 1, :, lanes], u[i + 1, :, lanes]], axis=1)
                    total += dot(around, middle[(i - 1) * plan.run + p])
                if p == half and i > 0:
                    total += dot(u[i - wrap, :, (half - 1) * width : half * width], spans[i])
                if p == half - 1 and i < last:
                    total += dot(u[i + wrap, :, half * width : (half + 1) * width], spans[plan.rows + i + wrap])
                result = (a * scale[pl.ds(i * plan.run + p, 1), :]) * total
                if b:
                    result += b * y[i, :, lanes]
                if has_before:
                    result += c * before[i, :, lanes]
                part[i, :, lanes] = result
    if gram:
        mass = refs[1 + has_before]
        total = jnp.zeros(mass.shape, F32)
        for i in range(plan.rows):
            rounded = y[i].astype(BF16)
            total += dot_turned(rounded, rounded)
        mass[...] = total


def inner(plan, factors, u, y, before, w_in, scale, gram=False):
    has_before = before is not None
    args = (u, y, *w_in, scale) + ((before,) if has_before else ())
    outs = (shape(plan.rows, plan.vectors, plan.lanes),)
    if gram:
        outs += (shape(plan.vectors, plan.vectors),)
    return call(
        "inner", functools.partial(inner_kernel, plan, factors, has_before, gram),
        outs,
        vm(len(args)),
        args,
        flops=130 << 20,
        moved=5 << 20,
    )


def halo_terms(plan, u, w_out, below, *gots):
    x, z, v, s = place(plan)
    even_layer, even_seg, wrap = lax.rem(z, 2) == 0, lax.rem(s, 2) == 0, s == 0
    width, half, last, at = plan.width, plan.half, plan.rows - 1, plan.outer
    got = dict(zip(ORDER, gots, strict=True))
    got_a, got_b, got_ring, got_core = got["a"], got["b"], got["ring"], got["core"]
    none = jnp.zeros(got_a.shape, BF16)
    top = lax.select(z == 0, none, lax.select(even_layer, got_b[...], got_a[...]))
    bottom = lax.select(z == plan.layers - 1, none, lax.select(even_layer, got_a[...], got_b[...]))
    left = [lax.select(even_seg, got_ring[i], got_core[i]) for i in range(plan.rows)]
    right = [lax.select(even_seg, got_core[i], got_ring[i]) for i in range(plan.rows)]

    def row(i):
        found = {0: dot(left[i], w_out[at["N", i, 0]])}
        found[plan.run - 1] = dot(right[i], w_out[at["N", i, plan.run]])

        def add(p, term):
            found[p] = found[p] + term if p in found else term

        if i == 0:
            for p in range(plan.run):
                add(p, dot(top[:, p * width : (p + 1) * width], w_out[at["F", 0, p]]))
            lanes = slice((half - 1) * width, half * width)
            before = lax.select(wrap, top[:, lanes], u[0, :, lanes])
            add(half, dot(before, w_out[at["N", 0, half]]))
        if i == last:
            for p in range(plan.run):
                add(p, dot(bottom[:, p * width : (p + 1) * width], below[1 + p]))
            lanes = slice(half * width, (half + 1) * width)
            after = lax.select(wrap, bottom[:, lanes], u[last, :, lanes])
            add(half - 1, dot(after, lax.select(wrap, below[0], w_out[at["N", last, half]])))
        return found

    return row


def finished_row(plan, i, part, scale, factor, terms):
    out = []
    for p in range(plan.run):
        value = part[i, :, p * plan.width : (p + 1) * plan.width]
        if p in terms:
            value += (factor * scale[pl.ds(i * plan.run + p, 1), :]) * terms[p]
        out.append(value)
    return out


def outer_kernel(plan, factor, leaving, part, u, w_out, below, scale, got_0, got_1, got_2, got_3, *refs):
    refs = list(refs)
    y_out, u_out, send_a, send_b, send_core, send_ring = refs[:6]
    row = halo_terms(plan, u, w_out, below, got_0, got_1, got_2, got_3)
    width = plan.width
    for i in range(plan.rows):
        values = finished_row(plan, i, part, scale, factor, row(i))
        for p, value in enumerate(values):
            y_out[i, :, p * width : (p + 1) * width] = value
            u_out[i, :, p * width : (p + 1) * width] = (scale[pl.ds(i * plan.run + p, 1), :] * value).astype(BF16)
    emit(plan, u_out, send_a, send_b, send_core, send_ring)
    if leaving:
        exit_core = refs[6]
        core = lax.rem(lax.axis_index("vec"), 2)
        for k in range(plan.segments // 2):
            half, chip = divmod(k, plan.vecs // 2)
            first = pl.multiple_of((2 * chip + 1 - core) * plan.columns, plan.columns)
            for r in range(plan.own):
                exit_core[k, r] = y_out[half * plan.own + r, pl.ds(first, plan.columns), :]


def exit_shape(plan, n):
    return shape(n, plan.own, plan.columns, plan.lanes)


def outer(plan, factor, part, u, w_out, scale, got, leaving=False):
    outs = (shape(plan.rows, plan.vectors, plan.lanes),) + sends(plan)
    if leaving:
        outs += (exit_shape(plan, plan.segments // 2),)
    args = (part, u, *w_out, scale) + tuple(got)
    return call(
        "outer", functools.partial(outer_kernel, plan, factor, leaving),
        outs,
        vm(len(args)),
        args,
        flops=40 << 20,
        moved=5 << 20,
    )


def leave_kernel(plan, y, got_core, *outs):
    x, z, v, s = place(plan)
    core, chip = lax.rem(v, 2), lax.div(v, 2)
    for (dx, dy), out in zip(chip_order(plan), outs, strict=True):
        at = chip_at(plan, x, chip, dx, dy)
        to_x = 1 - x if dx else x
        first = pl.multiple_of((2 * (at - to_x * (plan.vecs // 2)) + core) * plan.columns, plan.columns)
        for r in range(plan.own):
            out[0, r] = y[to_x * plan.own + r, pl.ds(first, plan.columns), :].astype(out.dtype)
            out[1, r] = got_core[at, r].astype(out.dtype)


def leave(plan, y, got_core):
    dims = (2, plan.own, plan.columns, plan.lanes)
    outs = tuple(shape(*dims, dtype=F32) for _ in chip_order(plan))
    return call("leave", functools.partial(leave_kernel, plan), outs, vm(2), (y, got_core), moved=4 << 20)


def gram_pieces(plan):
    rows = plan.vectors // plan.meshes
    height = 8 if rows % 8 == 0 else rows
    return rows, height, rows // height


def image_kernel(plan, part, u, w_out, below, scale, got_0, got_1, got_2, got_3, y, mass, out):
    row = halo_terms(plan, u, w_out, below, got_0, got_1, got_2, got_3)
    stiff = jnp.zeros((plan.vectors, plan.vectors), F32)
    for i in range(plan.rows):
        values = finished_row(plan, i, part, scale, 1.0, row(i))
        image = jnp.concatenate([value.astype(BF16) for value in values], axis=1)
        stiff += dot_turned(image, y[i].astype(BF16))
    rows, height, count = gram_pieces(plan)
    both = (stiff, mass[...])
    for m in range(plan.meshes):
        for v in range(plan.vecs):
            lanes = slice(v * plan.columns, (v + 1) * plan.columns)
            out[m * plan.vecs + v] = jnp.concatenate(
                [g[m * rows + h * height : m * rows + (h + 1) * height, lanes] for g in both for h in range(count)],
                axis=1,
            )


def image(plan, part, u, w_out, scale, got, y, mass):
    rows, height, count = gram_pieces(plan)
    args = (part, u, *w_out, scale) + tuple(got) + (y, mass)
    return call(
        "image", functools.partial(image_kernel, plan),
        shape(plan.meshes * plan.vecs, height, 2 * count * plan.columns),
        vm(len(args)),
        args,
        flops=50 << 20,
        moved=5 << 20,
    )


def sum_kernel(plan, got, stiff, mass):
    rows, height, count = gram_pieces(plan)
    total = jnp.sum(got[...], axis=0)
    for k, out in enumerate((stiff, mass)):
        for h in range(count):
            lo = (k * count + h) * plan.columns
            out[h * height : (h + 1) * height, :] = total[:, lo : lo + plan.columns]


def total(plan, grams):
    outs = (shape(gram_pieces(plan)[0], plan.columns),) * 2
    return call("total", functools.partial(sum_kernel, plan), outs, vm(1), (grams,), moved=1 << 17)


def arrive_kernel(plan, *refs):
    *gots, out = refs
    x, z, v, s = place(plan)
    for (dx, dy), got in zip(chip_order(plan), gots, strict=True):
        for other in range(2):
            seg = jnp.int32(0)
            for m in range(2):
                for at in range(plan.vecs):
                    source = plan.seg[m ^ dx, (at ^ other) ^ (2 * dy)]
                    seg = seg + jnp.where((x == m) & (v == at), source, 0)
            for r in range(plan.own):
                for p in range(plan.run):
                    to = pl.multiple_of((r * SPAN + column(plan, seg, p)) * plan.width, plan.width)
                    value = got[other, r, :, p * plan.width : (p + 1) * plan.width]
                    out[:, pl.ds(to, plan.width)] = value.astype(F32)


def arrive(plan, gots):
    out = shape(plan.columns, plan.blocks * plan.width)
    return call("arrive", functools.partial(arrive_kernel, plan), out, vm(len(gots)), tuple(gots), moved=2 << 20)


def shards(plan, panel, orient, mass, diag, near, far):
    w = plan.width
    panel = panel.T
    orient, mass = orient.reshape(plan.blocks, w), mass.reshape(plan.blocks, w)
    scale_own, entering, own_entering, first = prepare(plan, panel, orient, mass, diag, near, far)
    own_first, own_near, own_rest, others, rest, near_turned, far_turned = fetch(plan, diag, near, far)

    def half(m, v):
        return m ^ 1, v

    def spread(parts):
        found = []
        for (dx, dy), sent in zip(chip_order(plan), parts, strict=True):
            if dx or dy:
                sent = plan.swap(sent, lambda m, v, dx=dx, dy=dy: (m ^ dx, v ^ (2 * dy)))
            found.append(sent)
        return found

    first = plan.swap(first, half)
    parts = enter(plan, own_entering, plan.swap(entering, plan.core_swap))
    others, *parts = lax.optimization_barrier((others, *parts))
    gots = spread(parts)
    gots[0], rest = lax.optimization_barrier((gots[0], rest))
    others, rest = plan.swap(others, half), plan.swap(rest, half)
    n_above = plan.run + 1
    above = jnp.where(lax.axis_index("mesh") % 2 == 0, own_first[:n_above], first[:n_above])
    pairs = [(m * plan.vecs + v, (m - 2) * plan.vecs + v) for m in range(2, plan.meshes) for v in range(plan.vecs)]
    below = lax.ppermute(above, BOTH, pairs)

    y, scale, *field = begin(plan, gots, scale_own, first)
    *w_in, w_out = late(plan, own_first, own_near, own_rest, first, others, rest, near_turned, far_turned)
    w_out = (w_out, below)

    def exchange(field):
        u, a, b, core, ring = field
        got = {
            "a": lambda: plan.swap(a, plan.layer_a),
            "b": lambda: plan.swap(b, plan.layer_b),
            "ring": lambda: plan.swap(ring, plan.ring_swap),
            "core": lambda: plan.swap(core, plan.core_swap),
        }
        return u, tuple(got[name]() for name in ORDER)

    for application in range(APPS):
        before = None
        for step in range(DEGREE):
            factors = (2.0 / RADIUS, -2.0 * CENTER / RADIUS, -1.0) if step else (1.0 / RADIUS, -CENTER / RADIUS, 0.0)
            u, halos = exchange(field)
            (part,) = inner(plan, factors, u, y, before, w_in, scale)
            leaving = application == APPS - 1 and step == DEGREE - 1
            new, *field = outer(plan, factors[0], part, u, w_out, scale, halos, leaving)
            before, y = y, new
    *field, exit_core = field
    u, halos = exchange(field)
    part, mass_gram = inner(plan, (1.0, 0.0, 0.0), u, y, None, w_in, scale, gram=True)
    got_core = plan.swap(exit_core, plan.core_swap)
    part, got_core = lax.optimization_barrier((part, got_core))
    kept = spread(leave(plan, y, got_core))
    grams = image(plan, part, u, w_out, scale, halos, y, mass_gram)
    grams = lax.all_to_all(grams, BOTH, 0, 0, tiled=True)
    filtered = arrive(plan, kept)
    stiff_gram, mass_gram = total(plan, grams)
    return filtered.T, stiff_gram.T, mass_gram.T


def solution(mesh):
    placed = (P("mesh", "vec"), P("mesh"), P("mesh"), P("mesh"), P("mesh"), P("mesh"))

    def run(panel, orient, mass, diag, near, far):
        meshes, vecs = mesh.shape["mesh"], mesh.shape["vec"]
        plan = Plan(meshes, vecs, diag.shape[0] // meshes, diag.shape[1], panel.shape[1] // vecs)
        return jax.shard_map(
            functools.partial(shards, plan),
            mesh=mesh,
            in_specs=placed,
            out_specs=(P("mesh", "vec"), P("vec", "mesh"), P("vec", "mesh")),
            check_vma=False,
        )(panel, orient, mass, diag, near, far)

    return run
```

```python
import functools

import jax
import jax.numpy as jnp
from jax import lax
from jax.experimental import pallas as pl
from jax.experimental.pallas import tpu as pltpu
from jax.sharding import PartitionSpec as P

SPAN = 32
DEGREE = 4
APPS = 2
CENTER = 6.0
RADIUS = 8.0

BOTH = ("mesh", "vec")
ORDER = ("ring", "a", "b", "core")
F32 = jnp.float32
BF16 = jnp.bfloat16
VMEM_LIMIT = 24 * 1024 * 1024


def gray(t):
    return t ^ (t >> 1)


class Plan:
    def __init__(self, meshes, vecs, blocks, width, columns):
        self.meshes, self.vecs, self.blocks, self.width, self.columns = meshes, vecs, blocks, width, columns
        self.ring = [(0, gray(t)) for t in range(vecs)] + [(1, gray(t)) for t in reversed(range(vecs))]
        self.segments = 2 * vecs
        self.seg = {place: s for s, place in enumerate(self.ring)}
        self.layers = meshes // 2
        self.own = blocks // SPAN
        self.rows = 2 * self.own
        self.run = SPAN // self.segments
        self.half = self.run // 2
        self.lanes = self.run * width
        self.vectors = vecs * columns
        self.count = self.own * self.run
        self.first, self.rest, self.near = {("N", 0, self.half): 0}, {}, {}
        for p in range(self.run):
            self.first["F", 0, p] = len(self.first)
        for p in range(self.run + 1):
            self.first.setdefault(("N", 0, p), len(self.first))
        for r in range(1, self.own):
            for p in range(self.run + 1):
                self.near["N", r, p] = len(self.near)
            for p in range(self.run):
                self.rest["F", r, p] = len(self.rest)
        self.aux = len(self.first)
        self.n_rest = len(self.rest) + self.count // 2
        self.outer = {}
        for p in range(self.run):
            self.outer["F", 0, p] = len(self.outer)
        for i in range(self.rows):
            self.outer["N", i, 0] = len(self.outer)
            self.outer["N", i, self.run] = len(self.outer)
        for i in (0, self.rows - 1):
            self.outer["N", i, self.half] = len(self.outer)

    def swap(self, x, partner):
        pairs = []
        for m in range(self.meshes):
            for v in range(self.vecs):
                to, at = partner(m, v)
                pairs.append((m * self.vecs + v, to * self.vecs + at))
        return lax.ppermute(x, BOTH, pairs)

    def layer_a(self, m, v):
        to = m ^ 2
        return (to, v) if to < self.meshes else (m, v ^ 1)

    def layer_b(self, m, v):
        z = m // 2
        to = m + 2 if z % 2 else m - 2
        return (to, v) if 0 <= to < self.meshes else (m, v ^ 1)

    def ring_swap(self, m, v):
        s = self.seg[m % 2, v]
        x, at = self.ring[(s + 1) % self.segments if s % 2 else (s - 1) % self.segments]
        return m - m % 2 + x, at

    def core_swap(self, m, v):
        return m, v ^ 1


def place(plan):
    m, v = lax.axis_index("mesh"), lax.axis_index("vec")
    x, z = lax.rem(m, 2), lax.div(m, 2)
    s = jnp.int32(0)
    for k, (a, b) in enumerate(plan.ring):
        s = s + jnp.where((x == a) & (v == b), k, 0)
    return x, z, v, s


def column(plan, s, p):
    return lax.rem(plan.run * s + (p - plan.half + SPAN), SPAN)


def pieces(plan, s):
    found = []
    for p in range(plan.run):
        j = (plan.run * s + p - plan.half) % SPAN
        if found and found[-1][1] + found[-1][2] == j:
            found[-1][2] += 1
        else:
            found.append([p, j, 1])
    return found


def dot(u, w):
    return lax.dot_general(u, w, (((1,), (0,)), ((), ())), preferred_element_type=F32)


def dot_turned(u, w):
    return lax.dot_general(u, w, (((1,), (1,)), ((), ())), preferred_element_type=F32)


def call(name, kernel, outs, ins, args, scratch=(), flops=0, moved=0):
    return pl.pallas_call(
        kernel,
        name=name,
        out_shape=outs,
        in_specs=ins,
        out_specs=jax.tree.map(lambda _: pl.BlockSpec(memory_space=pltpu.VMEM), outs),
        scratch_shapes=list(scratch),
        compiler_params=pltpu.CompilerParams(vmem_limit_bytes=VMEM_LIMIT),
        cost_estimate=pl.CostEstimate(flops=flops, bytes_accessed=moved, transcendentals=0),
    )(*args)


def vm(n):
    return [pl.BlockSpec(memory_space=pltpu.VMEM)] * n


def in_hbm(n):
    return [pl.BlockSpec(memory_space=pltpu.HBM)] * n


def shape(*dims, dtype=F32):
    return jax.ShapeDtypeStruct(dims, dtype)


class Copies:
    def __init__(self, sems):
        self.sems, self.started = sems, []

    def start(self, src, dst):
        copy = pltpu.make_async_copy(src, dst, self.sems.at[len(self.started)])
        copy.start()
        self.started.append(copy)

    def start_one(self, first, src, dst, otherwise):
        sem = self.sems.at[len(self.started)]

        @pl.when(first)
        def _():
            pltpu.make_async_copy(src, dst, sem).start()

        @pl.when(jnp.logical_not(first))
        def _():
            pltpu.make_async_copy(src, otherwise, sem).start()

        self.started.append(pltpu.make_async_copy(src, dst, sem))

    def wait(self, lo=0, hi=None):
        for copy in self.started[lo:hi]:
            copy.wait()


def block_of(plan, src, seg, r, p):
    return src.at[r * SPAN + column(plan, seg, p)]


def upper(w):
    return lax.broadcasted_iota(jnp.int32, (w, w), 0) <= lax.broadcasted_iota(jnp.int32, (w, w), 1)


def on_diagonal(w):
    return lax.broadcasted_iota(jnp.int32, (w, w), 0) == lax.broadcasted_iota(jnp.int32, (w, w), 1)


def prepare_kernel(plan, panel, orient, mass, diag, near, far, scale, enter, own_enter, first, *scratch):
    signs, masses, blocks, parts, sems = scratch
    x, z, v, s = place(plan)
    other = plan.segments - 1 - s
    core = lax.rem(v, 2)
    copies = Copies(sems)
    copies.start(orient, signs)
    copies.start(mass, masses)
    for r in range(plan.own):
        for p in range(1, plan.run, 2):
            copies.start(block_of(plan, diag, other, r, p), blocks.at[(r * plan.run + p) // 2])
    for d in range(plan.segments):
        chip, at_core = divmod(d, 2)
        seg = plan.seg[d // plan.vecs, d % plan.vecs]
        for r in range(plan.own):
            for p, j, n in pieces(plan, seg):
                src = panel.at[:, pl.ds((r * SPAN + j) * plan.width, n * plan.width)]
                lanes = pl.ds(p * plan.width, n * plan.width)
                copies.start_one(core == at_core, src, own_enter.at[chip, r, :, lanes], enter.at[chip, r, :, lanes])
    for (kind, r, p), at in plan.first.items():
        copies.start(block_of(plan, near if kind == "N" else far, other, r, p), first.at[at])
    copies.wait(0, 2)
    scale[...] = signs[...].astype(F32) * lax.rsqrt(masses[...])
    parts[...] = jnp.zeros_like(parts)
    for r in range(plan.own):
        for p in range(plan.run):
            value = scale[pl.ds(r * SPAN + column(plan, other, p), 1), :]
            for part in range(3):
                rounded = value.astype(BF16).astype(F32)
                at = part * plan.count + r * plan.run + p
                parts[at : at + 1, :] = rounded
                value = value - rounded
    copies.wait(2, 2 + plan.count // 2)
    line = on_diagonal(plan.width)
    for k in range(plan.count // 2):
        at = 3 * plan.count + k
        parts[at : at + 1, :] = jnp.sum(jnp.where(line, blocks[k].astype(F32), 0.0), axis=0, keepdims=True)
    first[plan.aux] = parts[...].astype(BF16)
    copies.wait(2 + plan.count // 2)


def prepare(plan, panel, orient, mass, diag, near, far):
    w = plan.width
    n_copies = 2 + plan.count // 2 + len(plan.first)
    n_copies += plan.own * sum(len(pieces(plan, seg)) for seg in range(plan.segments))
    args = [pltpu.with_memory_space_constraint(a, pltpu.HBM) for a in (panel, orient, mass, diag, near, far)]
    entering = shape(plan.segments // 2, plan.own, plan.columns, plan.lanes)
    return call(
        "prepare",
        functools.partial(prepare_kernel, plan),
        (shape(plan.blocks, w), entering, entering, shape(plan.aux + 1, w, w, dtype=BF16)),
        in_hbm(6),
        args,
        [
            pltpu.VMEM((plan.blocks, w), orient.dtype),
            pltpu.VMEM((plan.blocks, w), F32),
            pltpu.VMEM((plan.count // 2, w, w), BF16),
            pltpu.VMEM((w, w), F32),
            pltpu.SemaphoreType.DMA((n_copies,)),
        ],
        moved=3 << 20,
    )


def turned(block):
    return block.astype(F32).T.astype(BF16)


def fetch_kernel(plan, diag, near, far, own_first, own_near, own_rest, others, rest, near_turned, far_turned, blocks, sems):
    x, z, v, s = place(plan)
    other = plan.segments - 1 - s
    copies = Copies(sems)
    for r in range(plan.own):
        for p in range(plan.run):
            copies.start(block_of(plan, diag, other, r, p), blocks.at[r * plan.run + p])
    for src, table, theirs, mine in ((near, plan.near, others, own_near), (far, plan.rest, rest, own_rest)):
        for (_, r, p), at in table.items():
            copies.start(block_of(plan, src, other, r, p), theirs.at[at])
            copies.start(block_of(plan, src, s, r, p), mine.at[at])
    for (kind, r, p), at in plan.first.items():
        copies.start(block_of(plan, near if kind == "N" else far, s, r, p), own_first.at[at])
    for r in range(plan.own):
        for p in range(plan.run):
            copies.start(block_of(plan, diag, s, r, p), own_rest.at[len(plan.rest) + r * plan.run + p])
    copies.wait(0, plan.count)
    keep = upper(plan.width)
    for k in range(plan.count // 2):
        one, two = blocks[2 * k].astype(F32), blocks[2 * k + 1].astype(F32)
        rest[len(plan.rest) + k] = jnp.where(keep, one, two).astype(BF16)
    copies.wait(plan.count)
    for r in range(plan.own):
        for p in range(plan.run):
            n, f = ("N", r, p), ("F", r, p)
            near_turned[r * plan.run + p] = turned(own_near[plan.near[n]] if r else own_first[plan.first[n]])
            far_turned[r * plan.run + p] = turned(own_rest[plan.rest[f]] if r else own_first[plan.first[f]])


def fetch(plan, diag, near, far):
    w = plan.width
    args = [pltpu.with_memory_space_constraint(a, pltpu.HBM) for a in (diag, near, far)]
    n_near, n_own = len(plan.near), len(plan.rest) + plan.count
    return call(
        "fetch",
        functools.partial(fetch_kernel, plan),
        tuple(shape(n, w, w, dtype=BF16) for n in (len(plan.first), n_near, n_own, n_near, plan.n_rest, plan.count, plan.count)),
        in_hbm(3),
        args,
        [
            pltpu.VMEM((plan.count, w, w), BF16),
            pltpu.SemaphoreType.DMA((plan.count + 2 * n_near + len(plan.rest) + len(plan.first) + n_own,)),
        ],
        moved=3 << 20,
    )


def enter_kernel(plan, own_enter, got_core, *outs):
    x, z, v, s = place(plan)
    core, chip = lax.rem(v, 2), lax.div(v, 2)
    for (dx, dy), out in zip(chip_order(plan), outs, strict=True):
        at = chip_at(plan, x, chip, dx, dy)
        for r in range(plan.own):
            out[core, r] = own_enter[at, r]
            out[1 - core, r] = got_core[at, r]


def enter(plan, own_enter, got_core):
    n = len(chip_order(plan))
    return call(
        "enter",
        functools.partial(enter_kernel, plan),
        (exit_shape(plan, 2),) * n,
        vm(2),
        (own_enter, got_core),
        moved=4 << 20,
    )


def chip_order(plan):
    pairs = [(dx, dy) for dx in range(2) for dy in range(plan.vecs // 2)]
    return pairs[plan.vecs // 2 :] + pairs[: plan.vecs // 2]


def chip_at(plan, x, chip, dx, dy):
    to_x = 1 - x if dx else x
    to_chip = chip
    if dy:
        to_chip = jnp.int32(0)
        for k in range(plan.vecs // 2):
            to_chip = to_chip + jnp.where(chip == k, k ^ dy, 0)
    return to_x * (plan.vecs // 2) + to_chip


def emit(plan, u, u_out, send_a, send_b, send_core, send_ring):
    x, z, v, s = place(plan)
    last, width = plan.rows - 1, plan.width
    even_layer, even_seg = lax.rem(z, 2) == 0, lax.rem(s, 2) == 0
    for i in range(plan.rows):
        for p in range(plan.run):
            u_out[i, :, p * width : (p + 1) * width] = u[i][p]
        send_core[i] = lax.select(even_seg, u[i][-1], u[i][0])
        send_ring[i] = lax.select(even_seg, u[i][0], u[i][-1])
    for p in range(plan.run):
        lanes = slice(p * width, (p + 1) * width)
        send_a[:, lanes] = lax.select(even_layer, u[last][p], u[0][p])
        send_b[:, lanes] = lax.select(even_layer, u[0][p], u[last][p])


def sends(plan):
    w = plan.width
    edge = shape(plan.vectors, plan.lanes, dtype=BF16)
    side = shape(plan.rows, plan.vectors, w, dtype=BF16)
    return (shape(plan.rows, plan.vectors, plan.lanes, dtype=BF16), edge, edge, side, side)


def begin_kernel(plan, scale_own, first, *refs):
    gots, refs = refs[: plan.vecs], refs[plan.vecs :]
    y_out, scale_out, u_out, send_a, send_b, send_core, send_ring = refs
    x, z, v, s = place(plan)
    count = plan.count
    parts = first[plan.aux].astype(F32)
    theirs = (parts[:count] + parts[count : 2 * count]) + parts[2 * count : 3 * count]
    chip = lax.div(v, 2)
    for (dx, dy), got in zip(chip_order(plan), gots, strict=True):
        from_x = 1 - x if dx else x
        from_chip = chip_at(plan, x, chip, dx, dy) - from_x * (plan.vecs // 2)
        for core in range(2):
            lo = pl.multiple_of((2 * from_chip + core) * plan.columns, plan.columns)
            for r in range(plan.own):
                y_out[from_x * plan.own + r, pl.ds(lo, plan.columns), :] = got[core, r]
    u = []
    for i in range(plan.rows):
        half, r = divmod(i, plan.own)
        for p in range(plan.run):
            mine = scale_own[pl.ds(r * SPAN + column(plan, s, p), 1), :]
            scale_out[pl.ds(i * plan.run + p, 1), :] = jnp.where(
                x == half, mine, theirs[r * plan.run + p : r * plan.run + p + 1]
            )
    for i in range(plan.rows):
        u.append([])
        for p in range(plan.run):
            row, lanes = scale_out[pl.ds(i * plan.run + p, 1), :], slice(p * plan.width, (p + 1) * plan.width)
            u[i].append((row * y_out[i, :, lanes]).astype(BF16))
    emit(plan, u, u_out, send_a, send_b, send_core, send_ring)


def begin(plan, gots, scale_own, first):
    return call(
        "begin", functools.partial(begin_kernel, plan),
        (shape(plan.rows, plan.vectors, plan.lanes), shape(plan.rows * plan.run, plan.width)) + sends(plan),
        vm(2 + len(gots)),
        (scale_own, first, *gots),
        moved=4 << 20,
    )


def late_kernel(
    plan, own_first, own_near, own_rest, first, others, rest, near_turned, far_turned, pairs, middle, ends, spans, outer
):
    x, _, _, _ = place(plan)
    w, last = plan.width, plan.rows - 1
    keep, line = upper(w), on_diagonal(w)
    diagonals = first[plan.aux].astype(F32)
    theirs = []
    for k in range(plan.count // 2):
        both = rest[len(plan.rest) + k].astype(F32)
        flipped = both.T
        at = 3 * plan.count + k
        theirs.append(jnp.where(keep, both, flipped).astype(BF16))
        theirs.append(jnp.where(line, diagonals[at : at + 1], jnp.where(keep, flipped, both)).astype(BF16))
    lo, hi = slice(0, w), slice(w, 2 * w)
    for half in range(2):

        @pl.when(x == half)
        def _():
            for i in range(plan.rows):
                group, r = divmod(i, plan.own)
                mine = group == half

                def block(kind, p):
                    key = kind, r, p
                    if r == 0:
                        return (own_first if mine else first)[plan.first[key]]
                    if kind == "N":
                        return (own_near if mine else others)[plan.near[key]]
                    return (own_rest if mine else rest)[plan.rest[key]]

                outer[plan.outer["N", i, plan.run]] = block("N", plan.run)
                for p in range(plan.run):
                    at, k, q = i * plan.run + p, (i * plan.run + p) // 2, p % 2
                    own = own_rest[len(plan.rest) + r * plan.run + p] if mine else theirs[r * plan.run + p]
                    pairs[k, (lo, hi)[q], (lo, hi)[q]] = own
                    near = block("N", p)
                    near_flipped = near_turned[r * plan.run + p] if mine else turned(near)
                    if q:
                        pairs[k, lo, hi] = near_flipped
                        pairs[k, hi, lo] = near
                    if p == 0:
                        outer[plan.outer["N", i, 0]] = near_flipped
                    if p == plan.half:
                        spans[i] = near_flipped
                        spans[plan.rows + i] = near
                        if i == 0:
                            outer[plan.outer["N", 0, p]] = near_flipped
                        if i == last:
                            outer[plan.outer["N", last, p]] = near
                    far = block("F", p)
                    far_flipped = far_turned[r * plan.run + p] if mine else turned(far)
                    if i == 0:
                        outer[plan.outer["F", 0, p]] = far_flipped
                    elif i == last:
                        ends[plan.run + p] = far_flipped
                    else:
                        middle[at - plan.run, lo] = far_flipped
                    if i == 1:
                        ends[p] = far
                    elif i > 1:
                        middle[at - 2 * plan.run, hi] = far


def late(plan, *args):
    w = plan.width
    return call(
        "late",
        functools.partial(late_kernel, plan),
        (
            shape(plan.rows * plan.run // 2, 2 * w, 2 * w, dtype=BF16),
            shape((plan.rows - 2) * plan.run, 2 * w, w, dtype=BF16),
            shape(2 * plan.run, w, w, dtype=BF16),
            shape(2 * plan.rows, w, w, dtype=BF16),
            shape(len(plan.outer), w, w, dtype=BF16),
        ),
        vm(len(args)),
        args,
        moved=4 << 20,
    )


def inner_kernel(plan, factors, has_before, gram, u, y, pairs, middle, ends, spans, scale, *refs):
    a, b, c = factors
    before = refs[0] if has_before else None
    part = refs[has_before]
    x, z, v, s = place(plan)
    wrap = (s == 0).astype(jnp.int32)
    width, half, last = plan.width, plan.half, plan.rows - 1
    for i in range(plan.rows):
        for k in range(plan.run // 2):
            two = dot(u[i, :, 2 * k * width : (2 * k + 2) * width], pairs[i * plan.run // 2 + k])
            for p in (2 * k, 2 * k + 1):
                lanes = slice(p * width, (p + 1) * width)
                total = two[:, (p % 2) * width : (p % 2 + 1) * width]
                if i == 0:
                    total += dot(u[1, :, lanes], ends[p])
                elif i == last:
                    total += dot(u[last - 1, :, lanes], ends[plan.run + p])
                else:
                    around = jnp.concatenate([u[i - 1, :, lanes], u[i + 1, :, lanes]], axis=1)
                    total += dot(around, middle[(i - 1) * plan.run + p])
                if p == half and i > 0:
                    total += dot(u[i - wrap, :, (half - 1) * width : half * width], spans[i])
                if p == half - 1 and i < last:
                    total += dot(u[i + wrap, :, half * width : (half + 1) * width], spans[plan.rows + i + wrap])
                result = (a * scale[pl.ds(i * plan.run + p, 1), :]) * total
                if b:
                    result += b * y[i, :, lanes]
                if has_before:
                    result += c * before[i, :, lanes]
                part[i, :, lanes] = result
    if gram:
        mass = refs[1 + has_before]
        total = jnp.zeros(mass.shape, F32)
        for i in range(plan.rows):
            rounded = y[i].astype(BF16)
            total += dot_turned(rounded, rounded)
        mass[...] = total


def inner(plan, factors, u, y, before, w_in, scale, gram=False):
    has_before = before is not None
    args = (u, y, *w_in, scale) + ((before,) if has_before else ())
    outs = (shape(plan.rows, plan.vectors, plan.lanes),)
    if gram:
        outs += (shape(plan.vectors, plan.vectors),)
    return call(
        "inner", functools.partial(inner_kernel, plan, factors, has_before, gram),
        outs,
        vm(len(args)),
        args,
        flops=130 << 20,
        moved=5 << 20,
    )


def halo_terms(plan, u, w_out, below, *gots):
    x, z, v, s = place(plan)
    even_layer, even_seg, wrap = lax.rem(z, 2) == 0, lax.rem(s, 2) == 0, s == 0
    width, half, last, at = plan.width, plan.half, plan.rows - 1, plan.outer
    got = dict(zip(ORDER, gots, strict=True))
    got_a, got_b, got_ring, got_core = got["a"], got["b"], got["ring"], got["core"]
    none = jnp.zeros(got_a.shape, BF16)
    top = lax.select(z == 0, none, lax.select(even_layer, got_b[...], got_a[...]))
    bottom = lax.select(z == plan.layers - 1, none, lax.select(even_layer, got_a[...], got_b[...]))
    left = [lax.select(even_seg, got_ring[i], got_core[i]) for i in range(plan.rows)]
    right = [lax.select(even_seg, got_core[i], got_ring[i]) for i in range(plan.rows)]

    def row(i):
        found = {0: dot(left[i], w_out[at["N", i, 0]])}
        found[plan.run - 1] = dot(right[i], w_out[at["N", i, plan.run]])

        def add(p, term):
            found[p] = found[p] + term if p in found else term

        if i == 0:
            for p in range(plan.run):
                add(p, dot(top[:, p * width : (p + 1) * width], w_out[at["F", 0, p]]))
            lanes = slice((half - 1) * width, half * width)
            before = lax.select(wrap, top[:, lanes], u[0, :, lanes])
            add(half, dot(before, w_out[at["N", 0, half]]))
        if i == last:
            for p in range(plan.run):
                add(p, dot(bottom[:, p * width : (p + 1) * width], below[1 + p]))
            lanes = slice(half * width, (half + 1) * width)
            after = lax.select(wrap, bottom[:, lanes], u[last, :, lanes])
            add(half - 1, dot(after, lax.select(wrap, below[0], w_out[at["N", last, half]])))
        return found

    return row


def finished_row(plan, i, part, scale, factor, terms):
    out = []
    for p in range(plan.run):
        value = part[i, :, p * plan.width : (p + 1) * plan.width]
        if p in terms:
            value += (factor * scale[pl.ds(i * plan.run + p, 1), :]) * terms[p]
        out.append(value)
    return out


def outer_kernel(plan, factor, leaving, part, u, w_out, below, scale, got_0, got_1, got_2, got_3, *refs):
    refs = list(refs)
    y_out, u_out, send_a, send_b, send_core, send_ring = refs[:6]
    row = halo_terms(plan, u, w_out, below, got_0, got_1, got_2, got_3)
    width = plan.width
    fields = []
    for i in range(plan.rows):
        values = finished_row(plan, i, part, scale, factor, row(i))
        fields.append([])
        for p, value in enumerate(values):
            y_out[i, :, p * width : (p + 1) * width] = value
            fields[i].append((scale[pl.ds(i * plan.run + p, 1), :] * value).astype(BF16))
    emit(plan, fields, u_out, send_a, send_b, send_core, send_ring)
    if leaving:
        exit_core = refs[6]
        core = lax.rem(lax.axis_index("vec"), 2)
        for k in range(plan.segments // 2):
            half, chip = divmod(k, plan.vecs // 2)
            first = pl.multiple_of((2 * chip + 1 - core) * plan.columns, plan.columns)
            for r in range(plan.own):
                exit_core[k, r] = y_out[half * plan.own + r, pl.ds(first, plan.columns), :]


def exit_shape(plan, n):
    return shape(n, plan.own, plan.columns, plan.lanes)


def outer(plan, factor, part, u, w_out, scale, got, leaving=False):
    outs = (shape(plan.rows, plan.vectors, plan.lanes),) + sends(plan)
    if leaving:
        outs += (exit_shape(plan, plan.segments // 2),)
    args = (part, u, *w_out, scale) + tuple(got)
    return call(
        "outer", functools.partial(outer_kernel, plan, factor, leaving),
        outs,
        vm(len(args)),
        args,
        flops=40 << 20,
        moved=5 << 20,
    )


def leave_kernel(plan, y, got_core, *outs):
    x, z, v, s = place(plan)
    core, chip = lax.rem(v, 2), lax.div(v, 2)
    for (dx, dy), out in zip(chip_order(plan), outs, strict=True):
        at = chip_at(plan, x, chip, dx, dy)
        to_x = 1 - x if dx else x
        first = pl.multiple_of((2 * (at - to_x * (plan.vecs // 2)) + core) * plan.columns, plan.columns)
        for r in range(plan.own):
            out[0, r] = y[to_x * plan.own + r, pl.ds(first, plan.columns), :].astype(out.dtype)
            out[1, r] = got_core[at, r].astype(out.dtype)


def leave(plan, y, got_core):
    dims = (2, plan.own, plan.columns, plan.lanes)
    outs = tuple(shape(*dims, dtype=F32) for _ in chip_order(plan))
    return call("leave", functools.partial(leave_kernel, plan), outs, vm(2), (y, got_core), moved=4 << 20)


def gram_pieces(plan):
    rows = plan.vectors // plan.meshes
    height = 8 if rows % 8 == 0 else rows
    return rows, height, rows // height


def image_kernel(plan, part, u, w_out, below, scale, got_0, got_1, got_2, got_3, y, mass, out):
    row = halo_terms(plan, u, w_out, below, got_0, got_1, got_2, got_3)
    stiff = jnp.zeros((plan.vectors, plan.vectors), F32)
    for i in range(plan.rows):
        values = finished_row(plan, i, part, scale, 1.0, row(i))
        image = jnp.concatenate([value.astype(BF16) for value in values], axis=1)
        stiff += dot_turned(image, y[i].astype(BF16))
    rows, height, count = gram_pieces(plan)
    both = (stiff, mass[...])
    for m in range(plan.meshes):
        for v in range(plan.vecs):
            lanes = slice(v * plan.columns, (v + 1) * plan.columns)
            out[m * plan.vecs + v] = jnp.concatenate(
                [g[m * rows + h * height : m * rows + (h + 1) * height, lanes] for g in both for h in range(count)],
                axis=1,
            )


def image(plan, part, u, w_out, scale, got, y, mass):
    rows, height, count = gram_pieces(plan)
    args = (part, u, *w_out, scale) + tuple(got) + (y, mass)
    return call(
        "image", functools.partial(image_kernel, plan),
        shape(plan.meshes * plan.vecs, height, 2 * count * plan.columns),
        vm(len(args)),
        args,
        flops=50 << 20,
        moved=5 << 20,
    )


def finish_kernel(plan, grams, *refs):
    *gots, out, stiff, mass = refs
    rows, height, count = gram_pieces(plan)
    total = jnp.sum(grams[...], axis=0)
    for k, gram in enumerate((stiff, mass)):
        for h in range(count):
            lo = (k * count + h) * plan.columns
            gram[h * height : (h + 1) * height, :] = total[:, lo : lo + plan.columns]
    x, z, v, s = place(plan)
    for (dx, dy), got in zip(chip_order(plan), gots, strict=True):
        for other in range(2):
            seg = jnp.int32(0)
            for m in range(2):
                for at in range(plan.vecs):
                    source = plan.seg[m ^ dx, (at ^ other) ^ (2 * dy)]
                    seg = seg + jnp.where((x == m) & (v == at), source, 0)
            for r in range(plan.own):
                for p in range(plan.run):
                    to = pl.multiple_of((r * SPAN + column(plan, seg, p)) * plan.width, plan.width)
                    value = got[other, r, :, p * plan.width : (p + 1) * plan.width]
                    out[:, pl.ds(to, plan.width)] = value.astype(F32)


def finish(plan, grams, gots):
    rows = gram_pieces(plan)[0]
    return call(
        "finish",
        functools.partial(finish_kernel, plan),
        (shape(plan.columns, plan.blocks * plan.width),) + (shape(rows, plan.columns),) * 2,
        vm(1 + len(gots)),
        (grams, *gots),
        moved=3 << 20,
    )


def shards(plan, panel, orient, mass, diag, near, far):
    w = plan.width
    panel = panel.T
    orient, mass = orient.reshape(plan.blocks, w), mass.reshape(plan.blocks, w)
    scale_own, entering, own_entering, first = prepare(plan, panel, orient, mass, diag, near, far)
    own_first, own_near, own_rest, others, rest, near_turned, far_turned = fetch(plan, diag, near, far)

    def half(m, v):
        return m ^ 1, v

    def spread(parts):
        found = []
        for (dx, dy), sent in zip(chip_order(plan), parts, strict=True):
            if dx or dy:
                sent = plan.swap(sent, lambda m, v, dx=dx, dy=dy: (m ^ dx, v ^ (2 * dy)))
            found.append(sent)
        return found

    first = plan.swap(first, half)
    parts = enter(plan, own_entering, plan.swap(entering, plan.core_swap))
    others, *parts = lax.optimization_barrier((others, *parts))
    gots = spread(parts)
    gots[0], rest = lax.optimization_barrier((gots[0], rest))
    others, rest = plan.swap(others, half), plan.swap(rest, half)
    n_above = plan.run + 1
    above = jnp.where(lax.axis_index("mesh") % 2 == 0, own_first[:n_above], first[:n_above])
    pairs = [(m * plan.vecs + v, (m - 2) * plan.vecs + v) for m in range(2, plan.meshes) for v in range(plan.vecs)]
    below = lax.ppermute(above, BOTH, pairs)

    y, scale, *field = begin(plan, gots, scale_own, first)
    *w_in, w_out = late(plan, own_first, own_near, own_rest, first, others, rest, near_turned, far_turned)
    w_out = (w_out, below)

    def exchange(field):
        u, a, b, core, ring = field
        got = {
            "a": lambda: plan.swap(a, plan.layer_a),
            "b": lambda: plan.swap(b, plan.layer_b),
            "ring": lambda: plan.swap(ring, plan.ring_swap),
            "core": lambda: plan.swap(core, plan.core_swap),
        }
        return u, tuple(got[name]() for name in ORDER)

    for application in range(APPS):
        before = None
        for step in range(DEGREE):
            factors = (2.0 / RADIUS, -2.0 * CENTER / RADIUS, -1.0) if step else (1.0 / RADIUS, -CENTER / RADIUS, 0.0)
            u, halos = exchange(field)
            (part,) = inner(plan, factors, u, y, before, w_in, scale)
            leaving = application == APPS - 1 and step == DEGREE - 1
            new, *field = outer(plan, factors[0], part, u, w_out, scale, halos, leaving)
            before, y = y, new
    *field, exit_core = field
    u, halos = exchange(field)
    part, mass_gram = inner(plan, (1.0, 0.0, 0.0), u, y, None, w_in, scale, gram=True)
    got_core = plan.swap(exit_core, plan.core_swap)
    part, got_core = lax.optimization_barrier((part, got_core))
    kept = spread(leave(plan, y, got_core))
    grams = image(plan, part, u, w_out, scale, halos, y, mass_gram)
    grams = lax.all_to_all(grams, BOTH, 0, 0, tiled=True)
    filtered, stiff_gram, mass_gram = finish(plan, grams, kept)
    return filtered.T, stiff_gram.T, mass_gram.T


def solution(mesh):
    placed = (P("mesh", "vec"), P("mesh"), P("mesh"), P("mesh"), P("mesh"), P("mesh"))

    def run(panel, orient, mass, diag, near, far):
        meshes, vecs = mesh.shape["mesh"], mesh.shape["vec"]
        plan = Plan(meshes, vecs, diag.shape[0] // meshes, diag.shape[1], panel.shape[1] // vecs)
        return jax.shard_map(
            functools.partial(shards, plan),
            mesh=mesh,
            in_specs=placed,
            out_specs=(P("mesh", "vec"), P("vec", "mesh"), P("vec", "mesh")),
            check_vma=False,
        )(panel, orient, mass, diag, near, far)

    return run
```

```python
import functools

import jax
import jax.numpy as jnp
from jax import lax
from jax.experimental import pallas as pl
from jax.experimental.pallas import tpu as pltpu
from jax.sharding import PartitionSpec as P

SPAN = 32
DEGREE = 4
APPS = 2
CENTER = 6.0
RADIUS = 8.0

BOTH = ("mesh", "vec")
ORDER = ("ring", "a", "b", "core")
F32 = jnp.float32
BF16 = jnp.bfloat16
VMEM_LIMIT = 24 * 1024 * 1024


def gray(t):
    return t ^ (t >> 1)


class Plan:
    def __init__(self, meshes, vecs, blocks, width, columns):
        self.meshes, self.vecs, self.blocks, self.width, self.columns = meshes, vecs, blocks, width, columns
        self.ring = [(0, gray(t)) for t in range(vecs)] + [(1, gray(t)) for t in reversed(range(vecs))]
        self.segments = 2 * vecs
        self.seg = {place: s for s, place in enumerate(self.ring)}
        self.layers = meshes // 2
        self.own = blocks // SPAN
        self.rows = 2 * self.own
        self.run = SPAN // self.segments
        self.half = self.run // 2
        self.lanes = self.run * width
        self.vectors = vecs * columns
        self.count = self.own * self.run
        self.first, self.rest, self.near = {("N", 0, self.half): 0}, {}, {}
        for p in range(self.run):
            self.first["F", 0, p] = len(self.first)
        for p in range(self.run + 1):
            self.first.setdefault(("N", 0, p), len(self.first))
        for r in range(1, self.own):
            for p in range(self.run + 1):
                self.near["N", r, p] = len(self.near)
            for p in range(self.run):
                self.rest["F", r, p] = len(self.rest)
        self.aux = len(self.first)
        self.n_rest = len(self.rest) + self.count // 2
        self.outer = {}
        for p in range(self.run):
            self.outer["F", 0, p] = len(self.outer)
        for i in range(self.rows):
            self.outer["N", i, 0] = len(self.outer)
            self.outer["N", i, self.run] = len(self.outer)
        for i in (0, self.rows - 1):
            self.outer["N", i, self.half] = len(self.outer)

    def swap(self, x, partner):
        pairs = []
        for m in range(self.meshes):
            for v in range(self.vecs):
                to, at = partner(m, v)
                pairs.append((m * self.vecs + v, to * self.vecs + at))
        return lax.ppermute(x, BOTH, pairs)

    def layer_a(self, m, v):
        to = m ^ 2
        return (to, v) if to < self.meshes else (m, v ^ 1)

    def layer_b(self, m, v):
        z = m // 2
        to = m + 2 if z % 2 else m - 2
        return (to, v) if 0 <= to < self.meshes else (m, v ^ 1)

    def ring_swap(self, m, v):
        s = self.seg[m % 2, v]
        x, at = self.ring[(s + 1) % self.segments if s % 2 else (s - 1) % self.segments]
        return m - m % 2 + x, at

    def core_swap(self, m, v):
        return m, v ^ 1


def place(plan):
    m, v = lax.axis_index("mesh"), lax.axis_index("vec")
    x, z = lax.rem(m, 2), lax.div(m, 2)
    s = jnp.int32(0)
    for k, (a, b) in enumerate(plan.ring):
        s = s + jnp.where((x == a) & (v == b), k, 0)
    return x, z, v, s


def column(plan, s, p):
    return lax.rem(plan.run * s + (p - plan.half + SPAN), SPAN)


def pieces(plan, s):
    found = []
    for p in range(plan.run):
        j = (plan.run * s + p - plan.half) % SPAN
        if found and found[-1][1] + found[-1][2] == j:
            found[-1][2] += 1
        else:
            found.append([p, j, 1])
    return found


def dot(u, w):
    return lax.dot_general(u, w, (((1,), (0,)), ((), ())), preferred_element_type=F32)


def dot_turned(u, w):
    return lax.dot_general(u, w, (((1,), (1,)), ((), ())), preferred_element_type=F32)


def call(name, kernel, outs, ins, args, scratch=(), flops=0, moved=0):
    return pl.pallas_call(
        kernel,
        name=name,
        out_shape=outs,
        in_specs=ins,
        out_specs=jax.tree.map(lambda _: pl.BlockSpec(memory_space=pltpu.VMEM), outs),
        scratch_shapes=list(scratch),
        compiler_params=pltpu.CompilerParams(vmem_limit_bytes=VMEM_LIMIT),
        cost_estimate=pl.CostEstimate(flops=flops, bytes_accessed=moved, transcendentals=0),
    )(*args)


def vm(n):
    return [pl.BlockSpec(memory_space=pltpu.VMEM)] * n


def in_hbm(n):
    return [pl.BlockSpec(memory_space=pltpu.HBM)] * n


def shape(*dims, dtype=F32):
    return jax.ShapeDtypeStruct(dims, dtype)


class Copies:
    def __init__(self, sems):
        self.sems, self.started = sems, []

    def start(self, src, dst):
        copy = pltpu.make_async_copy(src, dst, self.sems.at[len(self.started)])
        copy.start()
        self.started.append(copy)

    def start_one(self, first, src, dst, otherwise):
        sem = self.sems.at[len(self.started)]

        @pl.when(first)
        def _():
            pltpu.make_async_copy(src, dst, sem).start()

        @pl.when(jnp.logical_not(first))
        def _():
            pltpu.make_async_copy(src, otherwise, sem).start()

        self.started.append(pltpu.make_async_copy(src, dst, sem))

    def wait(self, lo=0, hi=None):
        for copy in self.started[lo:hi]:
            copy.wait()


def block_of(plan, src, seg, r, p):
    return src.at[r * SPAN + column(plan, seg, p)]


def upper(w):
    return lax.broadcasted_iota(jnp.int32, (w, w), 0) <= lax.broadcasted_iota(jnp.int32, (w, w), 1)


def on_diagonal(w):
    return lax.broadcasted_iota(jnp.int32, (w, w), 0) == lax.broadcasted_iota(jnp.int32, (w, w), 1)


def prepare_kernel(plan, panel, orient, mass, diag, near, far, scale, enter, own_enter, first, *scratch):
    signs, masses, blocks, parts, sems = scratch
    x, z, v, s = place(plan)
    other = plan.segments - 1 - s
    core = lax.rem(v, 2)
    copies = Copies(sems)
    copies.start(orient, signs)
    copies.start(mass, masses)
    for r in range(plan.own):
        for p in range(1, plan.run, 2):
            copies.start(block_of(plan, diag, other, r, p), blocks.at[(r * plan.run + p) // 2])
    for d in range(plan.segments):
        chip, at_core = divmod(d, 2)
        seg = plan.seg[d // plan.vecs, d % plan.vecs]
        for r in range(plan.own):
            for p, j, n in pieces(plan, seg):
                src = panel.at[:, pl.ds((r * SPAN + j) * plan.width, n * plan.width)]
                lanes = pl.ds(p * plan.width, n * plan.width)
                copies.start_one(core == at_core, src, own_enter.at[chip, r, :, lanes], enter.at[chip, r, :, lanes])
    for (kind, r, p), at in plan.first.items():
        copies.start(block_of(plan, near if kind == "N" else far, other, r, p), first.at[at])
    copies.wait(0, 2)
    scale[...] = signs[...].astype(F32) * lax.rsqrt(masses[...])
    parts[...] = jnp.zeros_like(parts)
    for r in range(plan.own):
        for p in range(plan.run):
            value = scale[pl.ds(r * SPAN + column(plan, other, p), 1), :]
            for part in range(3):
                rounded = value.astype(BF16).astype(F32)
                at = part * plan.count + r * plan.run + p
                parts[at : at + 1, :] = rounded
                value = value - rounded
    copies.wait(2, 2 + plan.count // 2)
    line = on_diagonal(plan.width)
    for k in range(plan.count // 2):
        at = 3 * plan.count + k
        parts[at : at + 1, :] = jnp.sum(jnp.where(line, blocks[k].astype(F32), 0.0), axis=0, keepdims=True)
    first[plan.aux] = parts[...].astype(BF16)
    copies.wait(2 + plan.count // 2)


def prepare(plan, panel, orient, mass, diag, near, far):
    w = plan.width
    n_copies = 2 + plan.count // 2 + len(plan.first)
    n_copies += plan.own * sum(len(pieces(plan, seg)) for seg in range(plan.segments))
    args = [pltpu.with_memory_space_constraint(a, pltpu.HBM) for a in (panel, orient, mass, diag, near, far)]
    entering = shape(plan.segments // 2, plan.own, plan.columns, plan.lanes)
    return call(
        "prepare",
        functools.partial(prepare_kernel, plan),
        (shape(plan.blocks, w), entering, entering, shape(plan.aux + 1, w, w, dtype=BF16)),
        in_hbm(6),
        args,
        [
            pltpu.VMEM((plan.blocks, w), orient.dtype),
            pltpu.VMEM((plan.blocks, w), F32),
            pltpu.VMEM((plan.count // 2, w, w), BF16),
            pltpu.VMEM((w, w), F32),
            pltpu.SemaphoreType.DMA((n_copies,)),
        ],
        moved=3 << 20,
    )


def turned(block):
    return block.astype(F32).T.astype(BF16)


def fetch_kernel(plan, diag, near, far, own_first, own_near, own_rest, others, rest, near_turned, far_turned, blocks, sems):
    x, z, v, s = place(plan)
    other = plan.segments - 1 - s
    copies = Copies(sems)
    for r in range(plan.own):
        for p in range(plan.run):
            copies.start(block_of(plan, diag, other, r, p), blocks.at[r * plan.run + p])
    for src, table, theirs, mine in ((near, plan.near, others, own_near), (far, plan.rest, rest, own_rest)):
        for (_, r, p), at in table.items():
            copies.start(block_of(plan, src, other, r, p), theirs.at[at])
            copies.start(block_of(plan, src, s, r, p), mine.at[at])
    for (kind, r, p), at in plan.first.items():
        copies.start(block_of(plan, near if kind == "N" else far, s, r, p), own_first.at[at])
    for r in range(plan.own):
        for p in range(plan.run):
            copies.start(block_of(plan, diag, s, r, p), own_rest.at[len(plan.rest) + r * plan.run + p])
    copies.wait(0, plan.count)
    keep = upper(plan.width)
    for k in range(plan.count // 2):
        one, two = blocks[2 * k].astype(F32), blocks[2 * k + 1].astype(F32)
        rest[len(plan.rest) + k] = jnp.where(keep, one, two).astype(BF16)
    copies.wait(plan.count)
    for r in range(plan.own):
        for p in range(plan.run):
            n, f = ("N", r, p), ("F", r, p)
            near_turned[r * plan.run + p] = turned(own_near[plan.near[n]] if r else own_first[plan.first[n]])
            far_turned[r * plan.run + p] = turned(own_rest[plan.rest[f]] if r else own_first[plan.first[f]])


def fetch(plan, diag, near, far):
    w = plan.width
    args = [pltpu.with_memory_space_constraint(a, pltpu.HBM) for a in (diag, near, far)]
    n_near, n_own = len(plan.near), len(plan.rest) + plan.count
    return call(
        "fetch",
        functools.partial(fetch_kernel, plan),
        tuple(shape(n, w, w, dtype=BF16) for n in (len(plan.first), n_near, n_own, n_near, plan.n_rest, plan.count, plan.count)),
        in_hbm(3),
        args,
        [
            pltpu.VMEM((plan.count, w, w), BF16),
            pltpu.SemaphoreType.DMA((plan.count + 2 * n_near + len(plan.rest) + len(plan.first) + n_own,)),
        ],
        moved=3 << 20,
    )


def enter_kernel(plan, own_enter, got_core, *outs):
    x, z, v, s = place(plan)
    core, chip = lax.rem(v, 2), lax.div(v, 2)
    for (dx, dy), out in zip(chip_order(plan), outs, strict=True):
        at = chip_at(plan, x, chip, dx, dy)
        for r in range(plan.own):
            out[core, r] = own_enter[at, r]
            out[1 - core, r] = got_core[at, r]


def enter(plan, own_enter, got_core):
    n = len(chip_order(plan))
    return call(
        "enter",
        functools.partial(enter_kernel, plan),
        (exit_shape(plan, 2),) * n,
        vm(2),
        (own_enter, got_core),
        moved=4 << 20,
    )


def chip_order(plan):
    pairs = [(dx, dy) for dx in range(2) for dy in range(plan.vecs // 2)]
    return pairs[plan.vecs // 2 :][::-1] + pairs[: plan.vecs // 2]


def chip_at(plan, x, chip, dx, dy):
    to_x = 1 - x if dx else x
    to_chip = chip
    if dy:
        to_chip = jnp.int32(0)
        for k in range(plan.vecs // 2):
            to_chip = to_chip + jnp.where(chip == k, k ^ dy, 0)
    return to_x * (plan.vecs // 2) + to_chip


def emit(plan, u, u_out, send_a, send_b, send_core, send_ring):
    x, z, v, s = place(plan)
    last, width = plan.rows - 1, plan.width
    even_layer, even_seg = lax.rem(z, 2) == 0, lax.rem(s, 2) == 0
    for i in range(plan.rows):
        for p in range(plan.run):
            u_out[i, :, p * width : (p + 1) * width] = u[i][p]
        send_core[i] = lax.select(even_seg, u[i][-1], u[i][0])
        send_ring[i] = lax.select(even_seg, u[i][0], u[i][-1])
    for p in range(plan.run):
        lanes = slice(p * width, (p + 1) * width)
        send_a[:, lanes] = lax.select(even_layer, u[last][p], u[0][p])
        send_b[:, lanes] = lax.select(even_layer, u[0][p], u[last][p])


def sends(plan):
    w = plan.width
    edge = shape(plan.vectors, plan.lanes, dtype=BF16)
    side = shape(plan.rows, plan.vectors, w, dtype=BF16)
    return (shape(plan.rows, plan.vectors, plan.lanes, dtype=BF16), edge, edge, side, side)


def begin_kernel(plan, scale_own, first, *refs):
    gots, refs = refs[: plan.vecs], refs[plan.vecs :]
    y_out, scale_out, u_out, send_a, send_b, send_core, send_ring = refs
    x, z, v, s = place(plan)
    count = plan.count
    parts = first[plan.aux].astype(F32)
    theirs = (parts[:count] + parts[count : 2 * count]) + parts[2 * count : 3 * count]
    chip = lax.div(v, 2)
    for (dx, dy), got in zip(chip_order(plan), gots, strict=True):
        from_x = 1 - x if dx else x
        from_chip = chip_at(plan, x, chip, dx, dy) - from_x * (plan.vecs // 2)
        for core in range(2):
            lo = pl.multiple_of((2 * from_chip + core) * plan.columns, plan.columns)
            for r in range(plan.own):
                y_out[from_x * plan.own + r, pl.ds(lo, plan.columns), :] = got[core, r]
    u = []
    for i in range(plan.rows):
        half, r = divmod(i, plan.own)
        for p in range(plan.run):
            mine = scale_own[pl.ds(r * SPAN + column(plan, s, p), 1), :]
            scale_out[pl.ds(i * plan.run + p, 1), :] = jnp.where(
                x == half, mine, theirs[r * plan.run + p : r * plan.run + p + 1]
            )
    for i in range(plan.rows):
        u.append([])
        for p in range(plan.run):
            row, lanes = scale_out[pl.ds(i * plan.run + p, 1), :], slice(p * plan.width, (p + 1) * plan.width)
            u[i].append((row * y_out[i, :, lanes]).astype(BF16))
    emit(plan, u, u_out, send_a, send_b, send_core, send_ring)


def begin(plan, gots, scale_own, first):
    return call(
        "begin", functools.partial(begin_kernel, plan),
        (shape(plan.rows, plan.vectors, plan.lanes), shape(plan.rows * plan.run, plan.width)) + sends(plan),
        vm(2 + len(gots)),
        (scale_own, first, *gots),
        moved=4 << 20,
    )


def late_kernel(
    plan, own_first, own_near, own_rest, first, others, rest, near_turned, far_turned, pairs, middle, ends, spans, outer
):
    x, _, _, _ = place(plan)
    w, last = plan.width, plan.rows - 1
    keep, line = upper(w), on_diagonal(w)
    diagonals = first[plan.aux].astype(F32)
    theirs = []
    for k in range(plan.count // 2):
        both = rest[len(plan.rest) + k].astype(F32)
        flipped = both.T
        at = 3 * plan.count + k
        theirs.append(jnp.where(keep, both, flipped).astype(BF16))
        theirs.append(jnp.where(line, diagonals[at : at + 1], jnp.where(keep, flipped, both)).astype(BF16))
    lo, hi = slice(0, w), slice(w, 2 * w)
    for half in range(2):

        @pl.when(x == half)
        def _():
            for i in range(plan.rows):
                group, r = divmod(i, plan.own)
                mine = group == half

                def block(kind, p):
                    key = kind, r, p
                    if r == 0:
                        return (own_first if mine else first)[plan.first[key]]
                    if kind == "N":
                        return (own_near if mine else others)[plan.near[key]]
                    return (own_rest if mine else rest)[plan.rest[key]]

                outer[plan.outer["N", i, plan.run]] = block("N", plan.run)
                for p in range(plan.run):
                    at, k, q = i * plan.run + p, (i * plan.run + p) // 2, p % 2
                    own = own_rest[len(plan.rest) + r * plan.run + p] if mine else theirs[r * plan.run + p]
                    pairs[k, (lo, hi)[q], (lo, hi)[q]] = own
                    near = block("N", p)
                    near_flipped = near_turned[r * plan.run + p] if mine else turned(near)
                    if q:
                        pairs[k, lo, hi] = near_flipped
                        pairs[k, hi, lo] = near
                    if p == 0:
                        outer[plan.outer["N", i, 0]] = near_flipped
                    if p == plan.half:
                        spans[i] = near_flipped
                        spans[plan.rows + i] = near
                        if i == 0:
                            outer[plan.outer["N", 0, p]] = near_flipped
                        if i == last:
                            outer[plan.outer["N", last, p]] = near
                    far = block("F", p)
                    far_flipped = far_turned[r * plan.run + p] if mine else turned(far)
                    if i == 0:
                        outer[plan.outer["F", 0, p]] = far_flipped
                    elif i == last:
                        ends[plan.run + p] = far_flipped
                    else:
                        middle[at - plan.run, lo] = far_flipped
                    if i == 1:
                        ends[p] = far
                    elif i > 1:
                        middle[at - 2 * plan.run, hi] = far


def late(plan, *args):
    w = plan.width
    return call(
        "late",
        functools.partial(late_kernel, plan),
        (
            shape(plan.rows * plan.run // 2, 2 * w, 2 * w, dtype=BF16),
            shape((plan.rows - 2) * plan.run, 2 * w, w, dtype=BF16),
            shape(2 * plan.run, w, w, dtype=BF16),
            shape(2 * plan.rows, w, w, dtype=BF16),
            shape(len(plan.outer), w, w, dtype=BF16),
        ),
        vm(len(args)),
        args,
        moved=4 << 20,
    )


def inner_kernel(plan, factors, has_before, gram, u, y, pairs, middle, ends, spans, scale, *refs):
    a, b, c = factors
    before = refs[0] if has_before else None
    part = refs[has_before]
    x, z, v, s = place(plan)
    wrap = (s == 0).astype(jnp.int32)
    width, half, last = plan.width, plan.half, plan.rows - 1
    for i in range(plan.rows):
        for k in range(plan.run // 2):
            two = dot(u[i, :, 2 * k * width : (2 * k + 2) * width], pairs[i * plan.run // 2 + k])
            for p in (2 * k, 2 * k + 1):
                lanes = slice(p * width, (p + 1) * width)
                total = two[:, (p % 2) * width : (p % 2 + 1) * width]
                if i == 0:
                    total += dot(u[1, :, lanes], ends[p])
                elif i == last:
                    total += dot(u[last - 1, :, lanes], ends[plan.run + p])
                else:
                    around = jnp.concatenate([u[i - 1, :, lanes], u[i + 1, :, lanes]], axis=1)
                    total += dot(around, middle[(i - 1) * plan.run + p])
                if p == half and i > 0:
                    total += dot(u[i - wrap, :, (half - 1) * width : half * width], spans[i])
                if p == half - 1 and i < last:
                    total += dot(u[i + wrap, :, half * width : (half + 1) * width], spans[plan.rows + i + wrap])
                result = (a * scale[pl.ds(i * plan.run + p, 1), :]) * total
                if b:
                    result += b * y[i, :, lanes]
                if has_before:
                    result += c * before[i, :, lanes]
                part[i, :, lanes] = result
    if gram:
        mass = refs[1 + has_before]
        total = jnp.zeros(mass.shape, F32)
        for i in range(plan.rows):
            rounded = y[i].astype(BF16)
            total += dot_turned(rounded, rounded)
        mass[...] = total


def inner(plan, factors, u, y, before, w_in, scale, gram=False):
    has_before = before is not None
    args = (u, y, *w_in, scale) + ((before,) if has_before else ())
    outs = (shape(plan.rows, plan.vectors, plan.lanes),)
    if gram:
        outs += (shape(plan.vectors, plan.vectors),)
    return call(
        "inner", functools.partial(inner_kernel, plan, factors, has_before, gram),
        outs,
        vm(len(args)),
        args,
        flops=130 << 20,
        moved=5 << 20,
    )


def halo_terms(plan, u, w_out, below, *gots):
    x, z, v, s = place(plan)
    even_layer, even_seg, wrap = lax.rem(z, 2) == 0, lax.rem(s, 2) == 0, s == 0
    width, half, last, at = plan.width, plan.half, plan.rows - 1, plan.outer
    got = dict(zip(ORDER, gots, strict=True))
    got_a, got_b, got_ring, got_core = got["a"], got["b"], got["ring"], got["core"]
    none = jnp.zeros(got_a.shape, BF16)
    top = lax.select(z == 0, none, lax.select(even_layer, got_b[...], got_a[...]))
    bottom = lax.select(z == plan.layers - 1, none, lax.select(even_layer, got_a[...], got_b[...]))
    left = [lax.select(even_seg, got_ring[i], got_core[i]) for i in range(plan.rows)]
    right = [lax.select(even_seg, got_core[i], got_ring[i]) for i in range(plan.rows)]

    def row(i):
        found = {0: dot(left[i], w_out[at["N", i, 0]])}
        found[plan.run - 1] = dot(right[i], w_out[at["N", i, plan.run]])

        def add(p, term):
            found[p] = found[p] + term if p in found else term

        if i == 0:
            for p in range(plan.run):
                add(p, dot(top[:, p * width : (p + 1) * width], w_out[at["F", 0, p]]))
            lanes = slice((half - 1) * width, half * width)
            before = lax.select(wrap, top[:, lanes], u[0, :, lanes])
            add(half, dot(before, w_out[at["N", 0, half]]))
        if i == last:
            for p in range(plan.run):
                add(p, dot(bottom[:, p * width : (p + 1) * width], below[1 + p]))
            lanes = slice(half * width, (half + 1) * width)
            after = lax.select(wrap, bottom[:, lanes], u[last, :, lanes])
            add(half - 1, dot(after, lax.select(wrap, below[0], w_out[at["N", last, half]])))
        return found

    return row


def finished_row(plan, i, part, scale, factor, terms):
    out = []
    for p in range(plan.run):
        value = part[i, :, p * plan.width : (p + 1) * plan.width]
        if p in terms:
            value += (factor * scale[pl.ds(i * plan.run + p, 1), :]) * terms[p]
        out.append(value)
    return out


def outer_kernel(plan, factor, leaving, part, u, w_out, below, scale, got_0, got_1, got_2, got_3, *refs):
    refs = list(refs)
    y_out, u_out, send_a, send_b, send_core, send_ring = refs[:6]
    row = halo_terms(plan, u, w_out, below, got_0, got_1, got_2, got_3)
    width = plan.width
    fields = []
    for i in range(plan.rows):
        values = finished_row(plan, i, part, scale, factor, row(i))
        fields.append([])
        for p, value in enumerate(values):
            y_out[i, :, p * width : (p + 1) * width] = value
            fields[i].append((scale[pl.ds(i * plan.run + p, 1), :] * value).astype(BF16))
    emit(plan, fields, u_out, send_a, send_b, send_core, send_ring)
    if leaving:
        exit_core = refs[6]
        core = lax.rem(lax.axis_index("vec"), 2)
        for k in range(plan.segments // 2):
            half, chip = divmod(k, plan.vecs // 2)
            first = pl.multiple_of((2 * chip + 1 - core) * plan.columns, plan.columns)
            for r in range(plan.own):
                exit_core[k, r] = y_out[half * plan.own + r, pl.ds(first, plan.columns), :]


def exit_shape(plan, n):
    return shape(n, plan.own, plan.columns, plan.lanes)


def outer(plan, factor, part, u, w_out, scale, got, leaving=False):
    outs = (shape(plan.rows, plan.vectors, plan.lanes),) + sends(plan)
    if leaving:
        outs += (exit_shape(plan, plan.segments // 2),)
    args = (part, u, *w_out, scale) + tuple(got)
    return call(
        "outer", functools.partial(outer_kernel, plan, factor, leaving),
        outs,
        vm(len(args)),
        args,
        flops=40 << 20,
        moved=5 << 20,
    )


def leave_kernel(plan, y, got_core, *outs):
    x, z, v, s = place(plan)
    core, chip = lax.rem(v, 2), lax.div(v, 2)
    for (dx, dy), out in zip(chip_order(plan), outs, strict=True):
        at = chip_at(plan, x, chip, dx, dy)
        to_x = 1 - x if dx else x
        first = pl.multiple_of((2 * (at - to_x * (plan.vecs // 2)) + core) * plan.columns, plan.columns)
        for r in range(plan.own):
            out[0, r] = y[to_x * plan.own + r, pl.ds(first, plan.columns), :].astype(out.dtype)
            out[1, r] = got_core[at, r].astype(out.dtype)


def leave(plan, y, got_core):
    dims = (2, plan.own, plan.columns, plan.lanes)
    outs = tuple(shape(*dims, dtype=F32) for _ in chip_order(plan))
    return call("leave", functools.partial(leave_kernel, plan), outs, vm(2), (y, got_core), moved=4 << 20)


def gram_pieces(plan):
    rows = plan.vectors // plan.meshes
    height = 8 if rows % 8 == 0 else rows
    return rows, height, rows // height


def image_kernel(plan, part, u, w_out, below, scale, got_0, got_1, got_2, got_3, y, mass, out):
    row = halo_terms(plan, u, w_out, below, got_0, got_1, got_2, got_3)
    stiff = jnp.zeros((plan.vectors, plan.vectors), F32)
    for i in range(plan.rows):
        values = finished_row(plan, i, part, scale, 1.0, row(i))
        image = jnp.concatenate([value.astype(BF16) for value in values], axis=1)
        stiff += dot_turned(image, y[i].astype(BF16))
    rows, height, count = gram_pieces(plan)
    both = (stiff, mass[...])
    for m in range(plan.meshes):
        for v in range(plan.vecs):
            lanes = slice(v * plan.columns, (v + 1) * plan.columns)
            out[m * plan.vecs + v] = jnp.concatenate(
                [g[m * rows + h * height : m * rows + (h + 1) * height, lanes] for g in both for h in range(count)],
                axis=1,
            )


def image(plan, part, u, w_out, scale, got, y, mass):
    rows, height, count = gram_pieces(plan)
    args = (part, u, *w_out, scale) + tuple(got) + (y, mass)
    return call(
        "image", functools.partial(image_kernel, plan),
        shape(plan.meshes * plan.vecs, height, 2 * count * plan.columns),
        vm(len(args)),
        args,
        flops=50 << 20,
        moved=5 << 20,
    )


def finish_kernel(plan, grams, *refs):
    *gots, out, stiff, mass = refs
    rows, height, count = gram_pieces(plan)
    total = jnp.sum(grams[...], axis=0)
    for k, gram in enumerate((stiff, mass)):
        for h in range(count):
            lo = (k * count + h) * plan.columns
            gram[h * height : (h + 1) * height, :] = total[:, lo : lo + plan.columns]
    x, z, v, s = place(plan)
    for (dx, dy), got in zip(chip_order(plan), gots, strict=True):
        for other in range(2):
            seg = jnp.int32(0)
            for m in range(2):
                for at in range(plan.vecs):
                    source = plan.seg[m ^ dx, (at ^ other) ^ (2 * dy)]
                    seg = seg + jnp.where((x == m) & (v == at), source, 0)
            for r in range(plan.own):
                for p in range(plan.run):
                    to = pl.multiple_of((r * SPAN + column(plan, seg, p)) * plan.width, plan.width)
                    value = got[other, r, :, p * plan.width : (p + 1) * plan.width]
                    out[:, pl.ds(to, plan.width)] = value.astype(F32)


def finish(plan, grams, gots):
    rows = gram_pieces(plan)[0]
    return call(
        "finish",
        functools.partial(finish_kernel, plan),
        (shape(plan.columns, plan.blocks * plan.width),) + (shape(rows, plan.columns),) * 2,
        vm(1 + len(gots)),
        (grams, *gots),
        moved=3 << 20,
    )


def shards(plan, panel, orient, mass, diag, near, far):
    w = plan.width
    panel = panel.T
    orient, mass = orient.reshape(plan.blocks, w), mass.reshape(plan.blocks, w)
    scale_own, entering, own_entering, first = prepare(plan, panel, orient, mass, diag, near, far)
    own_first, own_near, own_rest, others, rest, near_turned, far_turned = fetch(plan, diag, near, far)

    def half(m, v):
        return m ^ 1, v

    def spread(parts):
        found = []
        for (dx, dy), sent in zip(chip_order(plan), parts, strict=True):
            if dx or dy:
                sent = plan.swap(sent, lambda m, v, dx=dx, dy=dy: (m ^ dx, v ^ (2 * dy)))
            found.append(sent)
        return found

    first = plan.swap(first, half)
    parts = enter(plan, own_entering, plan.swap(entering, plan.core_swap))
    others, *parts = lax.optimization_barrier((others, *parts))
    gots = spread(parts)
    gots[1], rest = lax.optimization_barrier((gots[1], rest))
    others, rest = plan.swap(others, half), plan.swap(rest, half)
    n_above = plan.run + 1
    above = jnp.where(lax.axis_index("mesh") % 2 == 0, own_first[:n_above], first[:n_above])
    pairs = [(m * plan.vecs + v, (m - 2) * plan.vecs + v) for m in range(2, plan.meshes) for v in range(plan.vecs)]
    below = lax.ppermute(above, BOTH, pairs)

    y, scale, *field = begin(plan, gots, scale_own, first)
    *w_in, w_out = late(plan, own_first, own_near, own_rest, first, others, rest, near_turned, far_turned)
    w_out = (w_out, below)

    def exchange(field):
        u, a, b, core, ring = field
        got = {
            "a": lambda: plan.swap(a, plan.layer_a),
            "b": lambda: plan.swap(b, plan.layer_b),
            "ring": lambda: plan.swap(ring, plan.ring_swap),
            "core": lambda: plan.swap(core, plan.core_swap),
        }
        return u, tuple(got[name]() for name in ORDER)

    for application in range(APPS):
        before = None
        for step in range(DEGREE):
            factors = (2.0 / RADIUS, -2.0 * CENTER / RADIUS, -1.0) if step else (1.0 / RADIUS, -CENTER / RADIUS, 0.0)
            u, halos = exchange(field)
            (part,) = inner(plan, factors, u, y, before, w_in, scale)
            leaving = application == APPS - 1 and step == DEGREE - 1
            new, *field = outer(plan, factors[0], part, u, w_out, scale, halos, leaving)
            before, y = y, new
    *field, exit_core = field
    u, halos = exchange(field)
    part, mass_gram = inner(plan, (1.0, 0.0, 0.0), u, y, None, w_in, scale, gram=True)
    got_core = plan.swap(exit_core, plan.core_swap)
    part, got_core = lax.optimization_barrier((part, got_core))
    kept = spread(leave(plan, y, got_core))
    grams = image(plan, part, u, w_out, scale, halos, y, mass_gram)
    grams = lax.all_to_all(grams, BOTH, 0, 0, tiled=True)
    filtered, stiff_gram, mass_gram = finish(plan, grams, kept)
    return filtered.T, stiff_gram.T, mass_gram.T


def solution(mesh):
    placed = (P("mesh", "vec"), P("mesh"), P("mesh"), P("mesh"), P("mesh"), P("mesh"))

    def run(panel, orient, mass, diag, near, far):
        meshes, vecs = mesh.shape["mesh"], mesh.shape["vec"]
        plan = Plan(meshes, vecs, diag.shape[0] // meshes, diag.shape[1], panel.shape[1] // vecs)
        return jax.shard_map(
            functools.partial(shards, plan),
            mesh=mesh,
            in_specs=placed,
            out_specs=(P("mesh", "vec"), P("vec", "mesh"), P("vec", "mesh")),
            check_vma=False,
        )(panel, orient, mass, diag, near, far)

    return run
```

```python
import functools

import jax
import jax.numpy as jnp
from jax import lax
from jax.experimental import pallas as pl
from jax.experimental.pallas import tpu as pltpu
from jax.sharding import PartitionSpec as P

SPAN = 32
DEGREE = 4
APPS = 2
CENTER = 6.0
RADIUS = 8.0

BOTH = ("mesh", "vec")
ORDER = ("ring", "a", "b", "core")
F32 = jnp.float32
BF16 = jnp.bfloat16
VMEM_LIMIT = 24 * 1024 * 1024


def gray(t):
    return t ^ (t >> 1)


class Plan:
    def __init__(self, meshes, vecs, blocks, width, columns):
        self.meshes, self.vecs, self.blocks, self.width, self.columns = meshes, vecs, blocks, width, columns
        self.ring = [(0, gray(t)) for t in range(vecs)] + [(1, gray(t)) for t in reversed(range(vecs))]
        self.segments = 2 * vecs
        self.seg = {place: s for s, place in enumerate(self.ring)}
        self.layers = meshes // 2
        self.own = blocks // SPAN
        self.rows = 2 * self.own
        self.run = SPAN // self.segments
        self.half = self.run // 2
        self.lanes = self.run * width
        self.vectors = vecs * columns
        self.count = self.own * self.run
        self.first, self.rest, self.near = {("N", 0, self.half): 0}, {}, {}
        for p in range(self.run):
            self.first["F", 0, p] = len(self.first)
        for p in range(self.run + 1):
            self.first.setdefault(("N", 0, p), len(self.first))
        for r in range(1, self.own):
            for p in range(self.run + 1):
                self.near["N", r, p] = len(self.near)
            for p in range(self.run):
                self.rest["F", r, p] = len(self.rest)
        self.aux = len(self.first)
        self.n_rest = len(self.rest) + self.count // 2
        self.outer = {}
        for p in range(self.run):
            self.outer["F", 0, p] = len(self.outer)
        for i in range(self.rows):
            self.outer["N", i, 0] = len(self.outer)
            self.outer["N", i, self.run] = len(self.outer)
        for i in (0, self.rows - 1):
            self.outer["N", i, self.half] = len(self.outer)

    def swap(self, x, partner):
        pairs = []
        for m in range(self.meshes):
            for v in range(self.vecs):
                to, at = partner(m, v)
                pairs.append((m * self.vecs + v, to * self.vecs + at))
        return lax.ppermute(x, BOTH, pairs)

    def layer_a(self, m, v):
        to = m ^ 2
        return (to, v) if to < self.meshes else (m, v ^ 1)

    def layer_b(self, m, v):
        z = m // 2
        to = m + 2 if z % 2 else m - 2
        return (to, v) if 0 <= to < self.meshes else (m, v ^ 1)

    def ring_swap(self, m, v):
        s = self.seg[m % 2, v]
        x, at = self.ring[(s + 1) % self.segments if s % 2 else (s - 1) % self.segments]
        return m - m % 2 + x, at

    def core_swap(self, m, v):
        return m, v ^ 1


def place(plan):
    m, v = lax.axis_index("mesh"), lax.axis_index("vec")
    x, z = lax.rem(m, 2), lax.div(m, 2)
    s = jnp.int32(0)
    for k, (a, b) in enumerate(plan.ring):
        s = s + jnp.where((x == a) & (v == b), k, 0)
    return x, z, v, s


def column(plan, s, p):
    return lax.rem(plan.run * s + (p - plan.half + SPAN), SPAN)


def pieces(plan, s):
    found = []
    for p in range(plan.run):
        j = (plan.run * s + p - plan.half) % SPAN
        if found and found[-1][1] + found[-1][2] == j:
            found[-1][2] += 1
        else:
            found.append([p, j, 1])
    return found


def dot(u, w):
    return lax.dot_general(u, w, (((1,), (0,)), ((), ())), preferred_element_type=F32)


def dot_turned(u, w):
    return lax.dot_general(u, w, (((1,), (1,)), ((), ())), preferred_element_type=F32)


def call(name, kernel, outs, ins, args, scratch=(), flops=0, moved=0):
    return pl.pallas_call(
        kernel,
        name=name,
        out_shape=outs,
        in_specs=ins,
        out_specs=jax.tree.map(lambda _: pl.BlockSpec(memory_space=pltpu.VMEM), outs),
        scratch_shapes=list(scratch),
        compiler_params=pltpu.CompilerParams(vmem_limit_bytes=VMEM_LIMIT),
        cost_estimate=pl.CostEstimate(flops=flops, bytes_accessed=moved, transcendentals=0),
    )(*args)


def vm(n):
    return [pl.BlockSpec(memory_space=pltpu.VMEM)] * n


def in_hbm(n):
    return [pl.BlockSpec(memory_space=pltpu.HBM)] * n


def shape(*dims, dtype=F32):
    return jax.ShapeDtypeStruct(dims, dtype)


class Copies:
    def __init__(self, sems):
        self.sems, self.started = sems, []

    def start(self, src, dst):
        copy = pltpu.make_async_copy(src, dst, self.sems.at[len(self.started)])
        copy.start()
        self.started.append(copy)

    def start_one(self, first, src, dst, otherwise):
        sem = self.sems.at[len(self.started)]

        @pl.when(first)
        def _():
            pltpu.make_async_copy(src, dst, sem).start()

        @pl.when(jnp.logical_not(first))
        def _():
            pltpu.make_async_copy(src, otherwise, sem).start()

        self.started.append(pltpu.make_async_copy(src, dst, sem))

    def wait(self, lo=0, hi=None):
        for copy in self.started[lo:hi]:
            copy.wait()


def block_of(plan, src, seg, r, p):
    return src.at[r * SPAN + column(plan, seg, p)]


def upper(w):
    return lax.broadcasted_iota(jnp.int32, (w, w), 0) <= lax.broadcasted_iota(jnp.int32, (w, w), 1)


def on_diagonal(w):
    return lax.broadcasted_iota(jnp.int32, (w, w), 0) == lax.broadcasted_iota(jnp.int32, (w, w), 1)


def prepare_kernel(plan, panel, orient, mass, diag, near, far, scale, enter, own_enter, first, *scratch):
    signs, masses, blocks, parts, sems = scratch
    x, z, v, s = place(plan)
    other = plan.segments - 1 - s
    core = lax.rem(v, 2)
    copies = Copies(sems)
    copies.start(orient, signs)
    copies.start(mass, masses)
    for r in range(plan.own):
        for p in range(1, plan.run, 2):
            copies.start(block_of(plan, diag, other, r, p), blocks.at[(r * plan.run + p) // 2])
    for d in range(plan.segments):
        chip, at_core = divmod(d, 2)
        seg = plan.seg[d // plan.vecs, d % plan.vecs]
        for r in range(plan.own):
            for p, j, n in pieces(plan, seg):
                src = panel.at[:, pl.ds((r * SPAN + j) * plan.width, n * plan.width)]
                lanes = pl.ds(p * plan.width, n * plan.width)
                copies.start_one(core == at_core, src, own_enter.at[chip, r, :, lanes], enter.at[chip, r, :, lanes])
    for (kind, r, p), at in plan.first.items():
        copies.start(block_of(plan, near if kind == "N" else far, other, r, p), first.at[at])
    copies.wait(0, 2)
    scale[...] = signs[...].astype(F32) * lax.rsqrt(masses[...])
    parts[...] = jnp.zeros_like(parts)
    for r in range(plan.own):
        for p in range(plan.run):
            value = scale[pl.ds(r * SPAN + column(plan, other, p), 1), :]
            for part in range(3):
                rounded = value.astype(BF16).astype(F32)
                at = part * plan.count + r * plan.run + p
                parts[at : at + 1, :] = rounded
                value = value - rounded
    copies.wait(2, 2 + plan.count // 2)
    line = on_diagonal(plan.width)
    for k in range(plan.count // 2):
        at = 3 * plan.count + k
        parts[at : at + 1, :] = jnp.sum(jnp.where(line, blocks[k].astype(F32), 0.0), axis=0, keepdims=True)
    first[plan.aux] = parts[...].astype(BF16)
    copies.wait(2 + plan.count // 2)


def prepare(plan, panel, orient, mass, diag, near, far):
    w = plan.width
    n_copies = 2 + plan.count // 2 + len(plan.first)
    n_copies += plan.own * sum(len(pieces(plan, seg)) for seg in range(plan.segments))
    args = [pltpu.with_memory_space_constraint(a, pltpu.HBM) for a in (panel, orient, mass, diag, near, far)]
    entering = shape(plan.segments // 2, plan.own, plan.columns, plan.lanes)
    return call(
        "prepare",
        functools.partial(prepare_kernel, plan),
        (shape(plan.blocks, w), entering, entering, shape(plan.aux + 1, w, w, dtype=BF16)),
        in_hbm(6),
        args,
        [
            pltpu.VMEM((plan.blocks, w), orient.dtype),
            pltpu.VMEM((plan.blocks, w), F32),
            pltpu.VMEM((plan.count // 2, w, w), BF16),
            pltpu.VMEM((w, w), F32),
            pltpu.SemaphoreType.DMA((n_copies,)),
        ],
        moved=3 << 20,
    )


def turned(block):
    return block.astype(F32).T.astype(BF16)


def fetch_kernel(plan, diag, near, far, own_first, own_near, own_rest, others, rest, near_turned, far_turned, blocks, sems):
    x, z, v, s = place(plan)
    other = plan.segments - 1 - s
    copies = Copies(sems)
    for r in range(plan.own):
        for p in range(plan.run):
            copies.start(block_of(plan, diag, other, r, p), blocks.at[r * plan.run + p])
    for src, table, theirs, mine in ((near, plan.near, others, own_near), (far, plan.rest, rest, own_rest)):
        for (_, r, p), at in table.items():
            copies.start(block_of(plan, src, other, r, p), theirs.at[at])
            copies.start(block_of(plan, src, s, r, p), mine.at[at])
    for (kind, r, p), at in plan.first.items():
        copies.start(block_of(plan, near if kind == "N" else far, s, r, p), own_first.at[at])
    for r in range(plan.own):
        for p in range(plan.run):
            copies.start(block_of(plan, diag, s, r, p), own_rest.at[len(plan.rest) + r * plan.run + p])
    copies.wait(0, plan.count)
    keep = upper(plan.width)
    for k in range(plan.count // 2):
        one, two = blocks[2 * k].astype(F32), blocks[2 * k + 1].astype(F32)
        rest[len(plan.rest) + k] = jnp.where(keep, one, two).astype(BF16)
    copies.wait(plan.count)
    for r in range(plan.own):
        for p in range(plan.run):
            n, f = ("N", r, p), ("F", r, p)
            near_turned[r * plan.run + p] = turned(own_near[plan.near[n]] if r else own_first[plan.first[n]])
            far_turned[r * plan.run + p] = turned(own_rest[plan.rest[f]] if r else own_first[plan.first[f]])


def fetch(plan, diag, near, far):
    w = plan.width
    args = [pltpu.with_memory_space_constraint(a, pltpu.HBM) for a in (diag, near, far)]
    n_near, n_own = len(plan.near), len(plan.rest) + plan.count
    return call(
        "fetch",
        functools.partial(fetch_kernel, plan),
        tuple(shape(n, w, w, dtype=BF16) for n in (len(plan.first), n_near, n_own, n_near, plan.n_rest, plan.count, plan.count)),
        in_hbm(3),
        args,
        [
            pltpu.VMEM((plan.count, w, w), BF16),
            pltpu.SemaphoreType.DMA((plan.count + 2 * n_near + len(plan.rest) + len(plan.first) + n_own,)),
        ],
        moved=3 << 20,
    )


def enter_kernel(plan, own_enter, got_core, *outs):
    x, z, v, s = place(plan)
    core, chip = lax.rem(v, 2), lax.div(v, 2)
    for (dx, dy), out in zip(chip_order(plan), outs, strict=True):
        at = chip_at(plan, x, chip, dx, dy)
        for r in range(plan.own):
            out[core, r] = own_enter[at, r]
            out[1 - core, r] = got_core[at, r]


def enter(plan, own_enter, got_core):
    n = len(chip_order(plan))
    return call(
        "enter",
        functools.partial(enter_kernel, plan),
        (exit_shape(plan, 2),) * n,
        vm(2),
        (own_enter, got_core),
        moved=4 << 20,
    )


def chip_order(plan):
    pairs = [(dx, dy) for dx in range(2) for dy in range(plan.vecs // 2)]
    return pairs[plan.vecs // 2 :][::-1] + pairs[: plan.vecs // 2]


def chip_at(plan, x, chip, dx, dy):
    to_x = 1 - x if dx else x
    to_chip = chip
    if dy:
        to_chip = jnp.int32(0)
        for k in range(plan.vecs // 2):
            to_chip = to_chip + jnp.where(chip == k, k ^ dy, 0)
    return to_x * (plan.vecs // 2) + to_chip


def emit(plan, u, u_out, send_a, send_b, send_core, send_ring):
    x, z, v, s = place(plan)
    last, width = plan.rows - 1, plan.width
    even_layer, even_seg = lax.rem(z, 2) == 0, lax.rem(s, 2) == 0
    for i in range(plan.rows):
        for p in range(plan.run):
            u_out[i, :, p * width : (p + 1) * width] = u[i][p]
        send_core[i] = lax.select(even_seg, u[i][-1], u[i][0])
        send_ring[i] = lax.select(even_seg, u[i][0], u[i][-1])
    for p in range(plan.run):
        lanes = slice(p * width, (p + 1) * width)
        send_a[:, lanes] = lax.select(even_layer, u[last][p], u[0][p])
        send_b[:, lanes] = lax.select(even_layer, u[0][p], u[last][p])


def sends(plan):
    w = plan.width
    edge = shape(plan.vectors, plan.lanes, dtype=BF16)
    side = shape(plan.rows, plan.vectors, w, dtype=BF16)
    return (shape(plan.rows, plan.vectors, plan.lanes, dtype=BF16), edge, edge, side, side)


def begin_kernel(plan, scale_own, first, *refs):
    gots, refs = refs[: plan.vecs], refs[plan.vecs :]
    y_out, scale_out, u_out, send_a, send_b, send_core, send_ring = refs
    x, z, v, s = place(plan)
    count = plan.count
    parts = first[plan.aux].astype(F32)
    theirs = (parts[:count] + parts[count : 2 * count]) + parts[2 * count : 3 * count]
    chip = lax.div(v, 2)
    for (dx, dy), got in zip(chip_order(plan), gots, strict=True):
        from_x = 1 - x if dx else x
        from_chip = chip_at(plan, x, chip, dx, dy) - from_x * (plan.vecs // 2)
        for core in range(2):
            lo = pl.multiple_of((2 * from_chip + core) * plan.columns, plan.columns)
            for r in range(plan.own):
                y_out[from_x * plan.own + r, pl.ds(lo, plan.columns), :] = got[core, r]
    u = []
    for i in range(plan.rows):
        half, r = divmod(i, plan.own)
        for p in range(plan.run):
            mine = scale_own[pl.ds(r * SPAN + column(plan, s, p), 1), :]
            scale_out[pl.ds(i * plan.run + p, 1), :] = jnp.where(
                x == half, mine, theirs[r * plan.run + p : r * plan.run + p + 1]
            )
    for i in range(plan.rows):
        u.append([])
        for p in range(plan.run):
            row, lanes = scale_out[pl.ds(i * plan.run + p, 1), :], slice(p * plan.width, (p + 1) * plan.width)
            u[i].append((row * y_out[i, :, lanes]).astype(BF16))
    emit(plan, u, u_out, send_a, send_b, send_core, send_ring)


def begin(plan, gots, scale_own, first):
    return call(
        "begin", functools.partial(begin_kernel, plan),
        (shape(plan.rows, plan.vectors, plan.lanes), shape(plan.rows * plan.run, plan.width)) + sends(plan),
        vm(2 + len(gots)),
        (scale_own, first, *gots),
        moved=4 << 20,
    )


def late_kernel(
    plan, own_first, own_near, own_rest, first, others, rest, near_turned, far_turned, pairs, middle, ends, spans, outer
):
    x, _, _, _ = place(plan)
    w, last = plan.width, plan.rows - 1
    keep, line = upper(w), on_diagonal(w)
    diagonals = first[plan.aux].astype(F32)
    theirs = []
    for k in range(plan.count // 2):
        both = rest[len(plan.rest) + k].astype(F32)
        flipped = both.T
        at = 3 * plan.count + k
        theirs.append(jnp.where(keep, both, flipped).astype(BF16))
        theirs.append(jnp.where(line, diagonals[at : at + 1], jnp.where(keep, flipped, both)).astype(BF16))
    lo, hi = slice(0, w), slice(w, 2 * w)
    for half in range(2):

        @pl.when(x == half)
        def _():
            for i in range(plan.rows):
                group, r = divmod(i, plan.own)
                mine = group == half

                def block(kind, p):
                    key = kind, r, p
                    if r == 0:
                        return (own_first if mine else first)[plan.first[key]]
                    if kind == "N":
                        return (own_near if mine else others)[plan.near[key]]
                    return (own_rest if mine else rest)[plan.rest[key]]

                outer[plan.outer["N", i, plan.run]] = block("N", plan.run)
                for p in range(plan.run):
                    at, k, q = i * plan.run + p, (i * plan.run + p) // 2, p % 2
                    own = own_rest[len(plan.rest) + r * plan.run + p] if mine else theirs[r * plan.run + p]
                    pairs[k, (lo, hi)[q], (lo, hi)[q]] = own
                    near = block("N", p)
                    near_flipped = near_turned[r * plan.run + p] if mine else turned(near)
                    if q:
                        pairs[k, lo, hi] = near_flipped
                        pairs[k, hi, lo] = near
                    if p == 0:
                        outer[plan.outer["N", i, 0]] = near_flipped
                    if p == plan.half:
                        spans[i] = near_flipped
                        spans[plan.rows + i] = near
                        if i == 0:
                            outer[plan.outer["N", 0, p]] = near_flipped
                        if i == last:
                            outer[plan.outer["N", last, p]] = near
                    far = block("F", p)
                    far_flipped = far_turned[r * plan.run + p] if mine else turned(far)
                    if i == 0:
                        outer[plan.outer["F", 0, p]] = far_flipped
                    elif i == last:
                        ends[plan.run + p] = far_flipped
                    else:
                        middle[at - plan.run, lo] = far_flipped
                    if i == 1:
                        ends[p] = far
                    elif i > 1:
                        middle[at - 2 * plan.run, hi] = far


def late(plan, *args):
    w = plan.width
    return call(
        "late",
        functools.partial(late_kernel, plan),
        (
            shape(plan.rows * plan.run // 2, 2 * w, 2 * w, dtype=BF16),
            shape((plan.rows - 2) * plan.run, 2 * w, w, dtype=BF16),
            shape(2 * plan.run, w, w, dtype=BF16),
            shape(2 * plan.rows, w, w, dtype=BF16),
            shape(len(plan.outer), w, w, dtype=BF16),
        ),
        vm(len(args)),
        args,
        moved=4 << 20,
    )


def inner_kernel(plan, factors, has_before, gram, u, y, pairs, middle, ends, spans, scale, *refs):
    a, b, c = factors
    before = refs[0] if has_before else None
    part = refs[has_before]
    x, z, v, s = place(plan)
    wrap = (s == 0).astype(jnp.int32)
    width, half, last = plan.width, plan.half, plan.rows - 1
    for i in range(plan.rows):
        for k in range(plan.run // 2):
            two = dot(u[i, :, 2 * k * width : (2 * k + 2) * width], pairs[i * plan.run // 2 + k])
            for p in (2 * k, 2 * k + 1):
                lanes = slice(p * width, (p + 1) * width)
                total = two[:, (p % 2) * width : (p % 2 + 1) * width]
                if i == 0:
                    total += dot(u[1, :, lanes], ends[p])
                elif i == last:
                    total += dot(u[last - 1, :, lanes], ends[plan.run + p])
                else:
                    around = jnp.concatenate([u[i - 1, :, lanes], u[i + 1, :, lanes]], axis=1)
                    total += dot(around, middle[(i - 1) * plan.run + p])
                if p == half and i > 0:
                    total += dot(u[i - wrap, :, (half - 1) * width : half * width], spans[i])
                if p == half - 1 and i < last:
                    total += dot(u[i + wrap, :, half * width : (half + 1) * width], spans[plan.rows + i + wrap])
                result = (a * scale[pl.ds(i * plan.run + p, 1), :]) * total
                if b:
                    result += b * y[i, :, lanes]
                if has_before:
                    result += c * before[i, :, lanes]
                part[i, :, lanes] = result
    if gram:
        mass = refs[1 + has_before]
        total = jnp.zeros(mass.shape, F32)
        for i in range(plan.rows):
            rounded = y[i].astype(BF16)
            total += dot_turned(rounded, rounded)
        mass[...] = total


def inner(plan, factors, u, y, before, w_in, scale, gram=False):
    has_before = before is not None
    args = (u, y, *w_in, scale) + ((before,) if has_before else ())
    outs = (shape(plan.rows, plan.vectors, plan.lanes),)
    if gram:
        outs += (shape(plan.vectors, plan.vectors),)
    return call(
        "inner", functools.partial(inner_kernel, plan, factors, has_before, gram),
        outs,
        vm(len(args)),
        args,
        flops=130 << 20,
        moved=5 << 20,
    )


def halo_terms(plan, u, w_out, below, *gots):
    x, z, v, s = place(plan)
    even_layer, even_seg, wrap = lax.rem(z, 2) == 0, lax.rem(s, 2) == 0, s == 0
    width, half, last, at = plan.width, plan.half, plan.rows - 1, plan.outer
    got = dict(zip(ORDER, gots, strict=True))
    got_a, got_b, got_ring, got_core = got["a"], got["b"], got["ring"], got["core"]
    none = jnp.zeros(got_a.shape, BF16)
    top = lax.select(z == 0, none, lax.select(even_layer, got_b[...], got_a[...]))
    bottom = lax.select(z == plan.layers - 1, none, lax.select(even_layer, got_a[...], got_b[...]))
    left = [lax.select(even_seg, got_ring[i], got_core[i]) for i in range(plan.rows)]
    right = [lax.select(even_seg, got_core[i], got_ring[i]) for i in range(plan.rows)]

    def row(i):
        found = {0: dot(left[i], w_out[at["N", i, 0]])}
        found[plan.run - 1] = dot(right[i], w_out[at["N", i, plan.run]])

        def add(p, term):
            found[p] = found[p] + term if p in found else term

        if i == 0:
            for p in range(plan.run):
                add(p, dot(top[:, p * width : (p + 1) * width], w_out[at["F", 0, p]]))
            lanes = slice((half - 1) * width, half * width)
            before = lax.select(wrap, top[:, lanes], u[0, :, lanes])
            add(half, dot(before, w_out[at["N", 0, half]]))
        if i == last:
            for p in range(plan.run):
                add(p, dot(bottom[:, p * width : (p + 1) * width], below[1 + p]))
            lanes = slice(half * width, (half + 1) * width)
            after = lax.select(wrap, bottom[:, lanes], u[last, :, lanes])
            add(half - 1, dot(after, lax.select(wrap, below[0], w_out[at["N", last, half]])))
        return found

    return row


def finished_row(plan, i, part, scale, factor, terms):
    out = []
    for p in range(plan.run):
        value = part[i, :, p * plan.width : (p + 1) * plan.width]
        if p in terms:
            value += (factor * scale[pl.ds(i * plan.run + p, 1), :]) * terms[p]
        out.append(value)
    return out


def outer_kernel(plan, factor, leaving, part, u, w_out, below, scale, got_0, got_1, got_2, got_3, *refs):
    refs = list(refs)
    y_out, u_out, send_a, send_b, send_core, send_ring = refs[:6]
    row = halo_terms(plan, u, w_out, below, got_0, got_1, got_2, got_3)
    width = plan.width
    fields = []
    for i in range(plan.rows):
        values = finished_row(plan, i, part, scale, factor, row(i))
        fields.append([])
        for p, value in enumerate(values):
            y_out[i, :, p * width : (p + 1) * width] = value
            fields[i].append((scale[pl.ds(i * plan.run + p, 1), :] * value).astype(BF16))
    emit(plan, fields, u_out, send_a, send_b, send_core, send_ring)
    if leaving:
        exit_core = refs[6]
        core = lax.rem(lax.axis_index("vec"), 2)
        for k in range(plan.segments // 2):
            half, chip = divmod(k, plan.vecs // 2)
            first = pl.multiple_of((2 * chip + 1 - core) * plan.columns, plan.columns)
            for r in range(plan.own):
                exit_core[k, r] = y_out[half * plan.own + r, pl.ds(first, plan.columns), :]


def exit_shape(plan, n):
    return shape(n, plan.own, plan.columns, plan.lanes)


def outer(plan, factor, part, u, w_out, scale, got, leaving=False):
    outs = (shape(plan.rows, plan.vectors, plan.lanes),) + sends(plan)
    if leaving:
        outs += (exit_shape(plan, plan.segments // 2),)
    args = (part, u, *w_out, scale) + tuple(got)
    return call(
        "outer", functools.partial(outer_kernel, plan, factor, leaving),
        outs,
        vm(len(args)),
        args,
        flops=40 << 20,
        moved=5 << 20,
    )


def leave_kernel(plan, y, got_core, *outs):
    x, z, v, s = place(plan)
    core, chip = lax.rem(v, 2), lax.div(v, 2)
    for (dx, dy), out in zip(chip_order(plan), outs, strict=True):
        at = chip_at(plan, x, chip, dx, dy)
        to_x = 1 - x if dx else x
        first = pl.multiple_of((2 * (at - to_x * (plan.vecs // 2)) + core) * plan.columns, plan.columns)
        for r in range(plan.own):
            out[0, r] = y[to_x * plan.own + r, pl.ds(first, plan.columns), :].astype(out.dtype)
            out[1, r] = got_core[at, r].astype(out.dtype)


def leave(plan, y, got_core):
    dims = (2, plan.own, plan.columns, plan.lanes)
    outs = tuple(shape(*dims, dtype=F32) for _ in chip_order(plan))
    return call("leave", functools.partial(leave_kernel, plan), outs, vm(2), (y, got_core), moved=4 << 20)


def gram_pieces(plan):
    rows = plan.vectors // plan.meshes
    height = 8 if rows % 8 == 0 else rows
    return rows, height, rows // height


def image_kernel(plan, part, u, w_out, below, scale, got_0, got_1, got_2, got_3, y, mass, out):
    row = halo_terms(plan, u, w_out, below, got_0, got_1, got_2, got_3)
    stiff = jnp.zeros((plan.vectors, plan.vectors), F32)
    for i in range(plan.rows):
        values = finished_row(plan, i, part, scale, 1.0, row(i))
        image = jnp.concatenate([value.astype(BF16) for value in values], axis=1)
        stiff += dot_turned(image, y[i].astype(BF16))
    rows, height, count = gram_pieces(plan)
    both = (stiff, mass[...])
    for m in range(plan.meshes):
        for v in range(plan.vecs):
            lanes = slice(v * plan.columns, (v + 1) * plan.columns)
            out[m * plan.vecs + v] = jnp.concatenate(
                [g[m * rows + h * height : m * rows + (h + 1) * height, lanes] for g in both for h in range(count)],
                axis=1,
            )


def image(plan, part, u, w_out, scale, got, y, mass):
    rows, height, count = gram_pieces(plan)
    args = (part, u, *w_out, scale) + tuple(got) + (y, mass)
    return call(
        "image", functools.partial(image_kernel, plan),
        shape(plan.meshes * plan.vecs, height, 2 * count * plan.columns),
        vm(len(args)),
        args,
        flops=50 << 20,
        moved=5 << 20,
    )


def finish_kernel(plan, grams, *refs):
    *gots, out, stiff, mass = refs
    rows, height, count = gram_pieces(plan)
    total = jnp.sum(grams[...], axis=0)
    for k, gram in enumerate((stiff, mass)):
        for h in range(count):
            lo = (k * count + h) * plan.columns
            gram[h * height : (h + 1) * height, :] = total[:, lo : lo + plan.columns]
    x, z, v, s = place(plan)
    for (dx, dy), got in zip(chip_order(plan), gots, strict=True):
        for other in range(2):
            seg = jnp.int32(0)
            for m in range(2):
                for at in range(plan.vecs):
                    source = plan.seg[m ^ dx, (at ^ other) ^ (2 * dy)]
                    seg = seg + jnp.where((x == m) & (v == at), source, 0)
            for r in range(plan.own):
                for p in range(plan.run):
                    to = pl.multiple_of((r * SPAN + column(plan, seg, p)) * plan.width, plan.width)
                    value = got[other, r, :, p * plan.width : (p + 1) * plan.width]
                    out[:, pl.ds(to, plan.width)] = value.astype(F32)


def finish(plan, grams, gots):
    rows = gram_pieces(plan)[0]
    return call(
        "finish",
        functools.partial(finish_kernel, plan),
        (shape(plan.columns, plan.blocks * plan.width),) + (shape(rows, plan.columns),) * 2,
        vm(1 + len(gots)),
        (grams, *gots),
        moved=3 << 20,
    )


def shards(plan, panel, orient, mass, diag, near, far):
    w = plan.width
    panel = panel.T
    orient, mass = orient.reshape(plan.blocks, w), mass.reshape(plan.blocks, w)
    scale_own, entering, own_entering, first = prepare(plan, panel, orient, mass, diag, near, far)
    own_first, own_near, own_rest, others, rest, near_turned, far_turned = fetch(plan, diag, near, far)

    def half(m, v):
        return m ^ 1, v

    def spread(parts):
        found = []
        for (dx, dy), sent in zip(chip_order(plan), parts, strict=True):
            if dx or dy:
                sent = plan.swap(sent, lambda m, v, dx=dx, dy=dy: (m ^ dx, v ^ (2 * dy)))
            found.append(sent)
        return found

    first = plan.swap(first, half)
    parts = enter(plan, own_entering, plan.swap(entering, plan.core_swap))
    gots = spread(parts)
    gots[1], others, rest = lax.optimization_barrier((gots[1], others, rest))
    others, rest = plan.swap(others, half), plan.swap(rest, half)
    n_above = plan.run + 1
    above = jnp.where(lax.axis_index("mesh") % 2 == 0, own_first[:n_above], first[:n_above])
    pairs = [(m * plan.vecs + v, (m - 2) * plan.vecs + v) for m in range(2, plan.meshes) for v in range(plan.vecs)]
    below = lax.ppermute(above, BOTH, pairs)

    y, scale, *field = begin(plan, gots, scale_own, first)
    *w_in, w_out = late(plan, own_first, own_near, own_rest, first, others, rest, near_turned, far_turned)
    w_out = (w_out, below)

    def exchange(field):
        u, a, b, core, ring = field
        got = {
            "a": lambda: plan.swap(a, plan.layer_a),
            "b": lambda: plan.swap(b, plan.layer_b),
            "ring": lambda: plan.swap(ring, plan.ring_swap),
            "core": lambda: plan.swap(core, plan.core_swap),
        }
        return u, tuple(got[name]() for name in ORDER)

    for application in range(APPS):
        before = None
        for step in range(DEGREE):
            factors = (2.0 / RADIUS, -2.0 * CENTER / RADIUS, -1.0) if step else (1.0 / RADIUS, -CENTER / RADIUS, 0.0)
            u, halos = exchange(field)
            (part,) = inner(plan, factors, u, y, before, w_in, scale)
            leaving = application == APPS - 1 and step == DEGREE - 1
            new, *field = outer(plan, factors[0], part, u, w_out, scale, halos, leaving)
            before, y = y, new
    *field, exit_core = field
    u, halos = exchange(field)
    part, mass_gram = inner(plan, (1.0, 0.0, 0.0), u, y, None, w_in, scale, gram=True)
    got_core = plan.swap(exit_core, plan.core_swap)
    part, got_core = lax.optimization_barrier((part, got_core))
    kept = spread(leave(plan, y, got_core))
    grams = image(plan, part, u, w_out, scale, halos, y, mass_gram)
    grams = lax.all_to_all(grams, BOTH, 0, 0, tiled=True)
    filtered, stiff_gram, mass_gram = finish(plan, grams, kept)
    return filtered.T, stiff_gram.T, mass_gram.T


def solution(mesh):
    placed = (P("mesh", "vec"), P("mesh"), P("mesh"), P("mesh"), P("mesh"), P("mesh"))

    def run(panel, orient, mass, diag, near, far):
        meshes, vecs = mesh.shape["mesh"], mesh.shape["vec"]
        plan = Plan(meshes, vecs, diag.shape[0] // meshes, diag.shape[1], panel.shape[1] // vecs)
        return jax.shard_map(
            functools.partial(shards, plan),
            mesh=mesh,
            in_specs=placed,
            out_specs=(P("mesh", "vec"), P("vec", "mesh"), P("vec", "mesh")),
            check_vma=False,
        )(panel, orient, mass, diag, near, far)

    return run
```
